128 devices in a mesh: att: 8 (over x, core), ffn: 16 (over y, z).
Axes of the slice: x: 4, y: 4, z: 4, core: 2. Of those that a mesh axis runs over, the one named last changes fastest.
Arguments:
- hidden: bfloat16 [4096, 7168], P(('att', 'ffn')), may hold values from -6 to 6
- route: int32 [4096, 1], P(('att', 'ffn')), may hold values from 0 to 7; in each aligned block of 32 rows (0 to 31, 32 to 63, ...) at most 8 rows name the same one
- norm_gain: float32 [7168], replicated, may hold values from 0.1 to 1.9
- gate_weight: bfloat16 [8, 7168, 9216], P('att', None, 'ffn'), may hold values from -0.0625 to 0.0625
- up_weight: bfloat16 [8, 7168, 9216], P('att', None, 'ffn'), may hold values from -0.0625 to 0.0625
- down_weight: bfloat16 [8, 9216, 7168], P('att', 'ffn'), may hold values from -0.0625 to 0.0625
Outputs:
- updated: bfloat16 [4096, 7168], P(('att', 'ffn'))
The draws below stay inside these ranges and needn't reach their ends.
Inputs may be any that keep to these rules, and one draw needn't show every extreme that they name: `route`: among the 32 rows of one device no group is named by more than 8 rows.
All inputs are finite; a program needn't handle non-finite values.
Results may differ from the reference program's by a relative error of at most 0.014.
Values may be sent and summed in bfloat16 or wider, within the bound.
A program may use at most 128 MiB of HBM per device.

```python
import math
import jax
import jax.numpy as jnp
import numpy as np
from jax import lax

D = 7168
FF = 9216
ROWS = 32
GROUPS = 8
CAP = 8
ROWS_ALL = 4096
N_ATT = 8
N_FFN = 16


def shard_levels(own_key, shape, cuts, least, high):
    factor_of = 1.0
    for axis_at, shards_of in cuts:
        steps = jax.random.uniform(jax.random.fold_in(jax.random.fold_in(own_key, 6), axis_at), (shards_of,), jnp.float32, least / len(cuts), high / len(cuts))
        factor_of = factor_of * jnp.repeat(jnp.exp(steps), shape[axis_at] // shards_of).reshape((-1,) + (1,) * (len(shape) - 1 - axis_at))
    return factor_of


def assign_block(rng, own, number, rows, amount, top, bound, slope):
    order = jax.random.permutation(rng, amount)
    packed, ordinary = load_shares(amount, rows * top, bound, slope, True), load_shares(amount, rows * top, bound, slope, False)
    places = jnp.arange(amount)

    def named(lengths, rotation):
        used = int((lengths > 0).sum())
        fixed = max(1, used // 4)
        moved = fixed + (places - fixed + rotation * (used - fixed)) % max(1, amount - fixed)
        return jnp.zeros((amount,), jnp.int32).at[order[jnp.where(places < fixed, places, moved)]].set(jnp.asarray(lengths, jnp.int32))

    lengths = jnp.where(number % 4 == 0, named(packed, number // 4), named(ordinary, number - number // 4 - 1))
    mixed = jax.random.permutation(jax.random.fold_in(own, 3), amount)
    donor, taker = mixed[0:amount // 2 * 2:2], mixed[1:amount // 2 * 2:2]
    room = jnp.minimum(lengths[donor] - 1, bound - lengths[taker]) // 2
    room = jnp.where((donor == order[0]) | (taker == order[0]) | (lengths[taker] == 0), 0, jnp.maximum(room, 0))
    moved = jax.random.randint(jax.random.fold_in(own, 4), (amount // 2,), 0, 1 << 20) % (room + 1)
    lengths = lengths.at[donor].add(-moved).at[taker].add(moved)
    members = jnp.searchsorted(jnp.cumsum(lengths), jnp.arange(rows * top), side="right").astype(jnp.int32)
    grid = members.reshape(top, rows).T
    grid = grid[jax.random.permutation(jax.random.fold_in(own, 1), rows)]
    rotation = jax.random.randint(jax.random.fold_in(own, 2), (rows, 1), 0, top)
    return jnp.take_along_axis(grid, (jnp.arange(top)[None, :] + rotation) % top, axis=1)


def load_shares(amount, total, bound, lean, full):
    weights = [(1 << 20) // math.isqrt(grade ** lean) + 1 for grade in range(1, amount + 1)]
    largest = bound if full else min(bound, max(-(-total // amount), total * weights[0] // sum(weights)))
    least = 1 if total - largest >= amount - 1 else 0
    given, spare = [largest] + [least] * (amount - 1), total - largest - least * (amount - 1)
    while spare > 0:
        movable = [i for i in range(1, amount) if given[i] < largest] or [i for i in range(1, amount) if given[i] < bound]
        pool, left = sum([weights[i] for i in movable]), spare
        for i in movable:
            addition = min(bound - given[i], max(1, left * weights[i] // pool), spare)
            given[i] = given[i] + addition
            spare = spare - addition
    return np.array(given)


def scatter_about(key, dims, width, most, shards=(), kind=jnp.bfloat16):
    result = jax.random.normal(key, dims, jnp.float32) * width
    if len(shards) > 0:
        result = shard_levels(key, dims, shards, -0.22, 0.18) * result
    return jnp.clip(result, min=-most, max=most).astype(kind)


def setup_inputs(seed: int = 0) -> dict:
    arg_keys = jax.random.split(jax.random.key(seed), 7)
    hidden = scatter_about(arg_keys[0], (ROWS_ALL, D), 1.0, 6.0, ((0, 128),))
    route_keys = jax.random.split(jax.random.fold_in(arg_keys[1], 1), ROWS_ALL // ROWS)
    route_turns = jax.random.permutation(jax.random.fold_in(arg_keys[1], 3), ROWS_ALL // ROWS)
    route = jax.vmap(lambda own, number: assign_block(jax.random.fold_in(arg_keys[1], 2), own, number, ROWS, N_ATT, 1, CAP, 2))(route_keys, route_turns).reshape((ROWS_ALL, 1))
    norm_gain = jnp.clip(1.0 + 0.18 * jax.random.normal(arg_keys[2], (D,), jnp.float32), 0.1, 1.9)
    gate_weight = scatter_about(arg_keys[3], (GROUPS, D, FF), D ** -0.5, 0.0625, ((0, 8), (2, 16)))
    up_weight = scatter_about(arg_keys[4], (GROUPS, D, FF), D ** -0.5, 0.0625, ((0, 8), (2, 16)))
    down_weight = scatter_about(arg_keys[5], (GROUPS, FF, D), FF ** -0.5, 0.0625, ((0, 8), (1, 16)))
    return {"hidden": hidden, "route": route, "norm_gain": norm_gain, "gate_weight": gate_weight, "up_weight": up_weight, "down_weight": down_weight}


def reference(hidden, route, norm_gain, gate_weight, up_weight, down_weight):
    widened = hidden.astype(jnp.float32)
    normed = (widened * lax.rsqrt(lax.optimization_barrier(jnp.mean(widened * widened, axis=-1, keepdims=True)) + 1e-06) * norm_gain.astype(jnp.float32)).astype(jnp.bfloat16)
    device_count = N_ATT * N_FFN
    chosen = route[:, 0].astype(jnp.int32).reshape(device_count, ROWS)
    member = (chosen[:, :, None] == jnp.arange(GROUPS, dtype=jnp.int32)[None, None, :]).astype(jnp.int32)
    before = jnp.cumsum(member, axis=1) - member
    row_rank = lax.optimization_barrier(jnp.sum(before * member, axis=-1)).astype(jnp.int32)
    position = (jnp.arange(device_count, dtype=jnp.int32)[:, None] * CAP + row_rank).reshape(-1)
    flat_group = chosen.reshape(-1)
    buffers = jnp.zeros((GROUPS, device_count * CAP, D), jnp.bfloat16).at[flat_group, position].set(normed)
    shard_size = FF // N_FFN

    def group_ffn(pieces):
        rows_in, w_gate, w_up, w_down = pieces
        gate_act = jnp.dot(rows_in, w_gate, preferred_element_type=jnp.float32)
        up_act = jnp.dot(rows_in, w_up, preferred_element_type=jnp.float32)
        mid_act = (jax.nn.silu(gate_act) * up_act).astype(jnp.bfloat16)
        accumulated = jnp.zeros((rows_in.shape[0], D), jnp.float32)
        for shard_idx in range(N_FFN):
            lower = shard_idx * shard_size
            term_part = jnp.dot(mid_act[:, lower:lower + shard_size], w_down[lower:lower + shard_size], preferred_element_type=jnp.float32).astype(jnp.bfloat16)
            accumulated = accumulated + lax.optimization_barrier(term_part).astype(jnp.float32)
        return accumulated.astype(jnp.bfloat16)
    results = lax.map(group_ffn, (buffers, gate_weight, up_weight, down_weight))
    ffn_rows = lax.optimization_barrier(results[flat_group, position])
    return (widened + ffn_rows.astype(jnp.float32)).astype(jnp.bfloat16)
```

```python
import jax
import jax.numpy as jnp
from jax import lax
from jax.experimental import pallas as pl
from jax.experimental.pallas import tpu as pltpu
from jax.sharding import PartitionSpec as P

MESH = pl.DeviceIdType.MESH
F32 = jnp.float32
BF16 = jnp.bfloat16


def chip_offset(part):
    return part + part // 2 - 2 * (part // 3)


def ffn_kernel(
    hidden, route, gain, gate_hbm, up_hbm, down_hbm, out,
    w_gate, w_up, w_down, blocks_out, blocks_in, blocks_back, returned, rows, gate_sum, up_sum, mid,
    near_y1, near_z1, near_y2, near_z2, far_z1, far_y1, far_z2, far_y2,
    w_sem, in_send, in_recv, back_send, back_recv, gather_send, gather_recv, reduce_send, reduce_recv,
):
    att, ffn = lax.axis_index("att"), lax.axis_index("ffn")
    x, core = att // 2, att % 2
    y, z = ffn // 4, ffn % 4
    yp, y2, ym = (y + 1) % 4, (y + 2) % 4, (y + 3) % 4
    zp, z2, zm = (z + 1) % 4, (z + 2) % 4, (z + 3) % 4
    width = hidden.shape[1]
    half, quarter = width // 2, width // 4
    a_cols, b_cols = pl.ds(0, half), pl.ds(half, half)
    q = [pl.ds(i * quarter, quarter) for i in range(4)]
    z_plus, z_minus, y_plus, y_minus = (att, y * 4 + zp), (att, y * 4 + zm), (att, yp * 4 + z), (att, ym * 4 + z)
    ALL = pl.ds(0, 4)

    barrier = pltpu.get_barrier_semaphore()
    for other in (z_plus, z_minus, y_plus, y_minus):
        pl.semaphore_signal(barrier, inc=1, device_id=other, device_id_type=MESH)
    for step in range(1, 8):
        pl.semaphore_signal(barrier, inc=1, device_id=((att + step) % 8, ffn), device_id_type=MESH)
    loads = [
        pltpu.make_async_copy(src.at[0], dst, w_sem.at[i])
        for i, (src, dst) in enumerate(((gate_hbm, w_gate), (up_hbm, w_up), (down_hbm, w_down)))
    ]
    for load in loads:
        load.start()

    widened = hidden[...].astype(F32)
    scale = lax.rsqrt(jnp.mean(widened * widened, axis=-1, keepdims=True) + 1e-06)
    normed = (widened * scale * gain[...]).astype(BF16)
    lane = lax.broadcasted_iota(jnp.int32, (32, 128), 1)
    member = (lane == route[...]).astype(F32)
    earlier = (
        lax.broadcasted_iota(jnp.int32, (32, 32), 1) < lax.broadcasted_iota(jnp.int32, (32, 32), 0)
    ).astype(F32)
    before = jnp.dot(earlier, member, preferred_element_type=F32)
    rank = jnp.sum(before * member, axis=1, keepdims=True).astype(jnp.int32)
    place = route[...] * 16 + rank
    table_a = (lane == place).astype(F32).astype(BF16)
    table_b = (lane == place + 8).astype(F32).astype(BF16)
    turned = (((0,), (0,)), ((), ()))
    placed = lax.dot_general(table_a, normed[:, :half], turned, preferred_element_type=F32)
    placed = placed + lax.dot_general(table_b, normed[:, half:], turned, preferred_element_type=F32)
    blocks_out[...] = placed.astype(BF16).reshape(8, 16, half)

    pl.semaphore_wait(barrier, 11)

    def in_copy(part, to_core):
        dest = ((x + 4 - chip_offset(part)) % 4) * 2 + to_core
        return pltpu.make_async_remote_copy(
            src_ref=blocks_out.at[dest], dst_ref=blocks_in.at[part, core],
            send_sem=in_send.at[part, to_core], recv_sem=in_recv.at[part, core],
            device_id=(dest, ffn), device_id_type=MESH,
        )

    in_copy(0, 1 - core).start()
    for part in range(1, 4):
        for to_core in range(2):
            in_copy(part, to_core).start()
    blocks_in[0, core] = blocks_out[att]

    def wait_in(part, from_core):
        pltpu.make_async_copy(blocks_out.at[0], blocks_in.at[part, from_core], in_recv.at[part, from_core]).wait()

    LINK = {0: z_plus, 1: z_minus, 2: y_plus, 3: y_minus}

    def g_send(part, link, event, at_y, at_z, cols):
        piece = rows.at[part, at_y, at_z, :, cols]
        pltpu.make_async_remote_copy(
            src_ref=piece, dst_ref=piece,
            send_sem=gather_send.at[part, event], recv_sem=gather_recv.at[part, link, event],
            device_id=LINK[link], device_id_type=MESH,
        ).start()

    def g_wait(part, link, event, cols):
        piece = rows.at[part, 0, 0, :, cols]
        pltpu.make_async_copy(piece, piece, gather_recv.at[part, link, event]).wait()

    whole = pl.ds(0, width)

    def gather_own(part):
        @pl.when(part == 0)
        def _():
            wait_in(0, 1 - core)

        @pl.when(part > 0)
        def _():
            wait_in(part, 0)
            wait_in(part, 1)

        first, second = blocks_in[part, 0].astype(F32), blocks_in[part, 1].astype(F32)
        rows[part, y, z, :, a_cols] = jnp.concatenate([first[:8], second[:8]], axis=0).astype(BF16)
        rows[part, y, z, :, b_cols] = jnp.concatenate([first[8:], second[8:]], axis=0).astype(BF16)
        for link in range(4):
            g_send(part, link, 0, y, z, whole)

    def gather_a(part):
        for link in range(4):
            g_wait(part, link, 0, whole)
        g_send(part, 0, 1, y, zm, q[0])
        g_send(part, 1, 1, y, zp, q[1])
        g_send(part, 2, 1, ym, z, q[2])
        g_send(part, 3, 1, yp, z, q[3])
        for link in (2, 3):
            g_send(part, link, 2, y, zm, a_cols)
        for link in (0, 1):
            g_send(part, link, 2, ym, z, b_cols)
        for link in (2, 3):
            g_send(part, link, 3, y, zp, a_cols)
        for link in (0, 1):
            g_send(part, link, 3, yp, z, b_cols)
        g_send(part, 0, 5, y, zm, q[2])
        g_send(part, 1, 5, y, zp, q[3])
        g_send(part, 2, 5, ym, z, q[0])
        g_send(part, 3, 5, yp, z, q[1])

    def gather_b(part):
        for link in range(4):
            g_wait(part, link, 1, q[0])
        for link in (2, 3):
            g_send(part, link, 4, y, z2, a_cols)
        for link in (0, 1):
            g_send(part, link, 4, y2, z, b_cols)

    def gather_on(part, event, of_y, of_z):
        for link in range(4):
            g_wait(part, link, event, a_cols)
        g_send(part, 0, event + 4, of_y, zm, q[2])
        g_send(part, 1, event + 4, of_y, zp, q[3])
        g_send(part, 2, event + 4, ym, of_z, q[0])
        g_send(part, 3, event + 4, yp, of_z, q[1])

    def gather_c(part):
        gather_on(part, 2, ym, zm)
        gather_on(part, 3, yp, zp)

    def gather_d(part):
        gather_on(part, 4, y2, z2)

    def gather_e(part):
        for event in range(5, 9):
            for link in range(4):
                g_wait(part, link, event, q[0])

    def wait_units(sem, part, units):
        piece = rows.at[part, 0, pl.ds(0, units)] if units <= 4 else rows.at[part, pl.ds(0, units // 4)]
        pltpu.make_async_copy(piece, piece, sem).wait()

    def gather_sent(part):
        for event, units in enumerate((4, 1, 2, 2, 2, 1, 1, 1, 1)):
            wait_units(gather_send.at[part, event], part, units)

    def project(part, lower, upper):
        @pl.loop(lower, upper)
        def _(i):
            cols = pl.ds(pl.multiple_of(i * quarter, quarter), quarter)
            block = rows[part, :, :, :, cols].reshape(256, quarter)
            gate = jnp.dot(block, w_gate[cols, :], preferred_element_type=F32)
            up = jnp.dot(block, w_up[cols, :], preferred_element_type=F32)

            @pl.when(i == 0)
            def _():
                gate_sum[...] = gate
                up_sum[...] = up

            @pl.when(i > 0)
            def _():
                gate_sum[...] += gate
                up_sum[...] += up

    def activate():
        gate = gate_sum[...]
        mid[...] = (gate / (1.0 + jnp.exp(-gate)) * up_sum[...]).astype(BF16)

    def lower_rows(part, lower, upper):
        @pl.loop(lower, upper)
        def _(i):
            cols = pl.ds(pl.multiple_of(i * quarter, quarter), quarter)
            partial = jnp.dot(mid[...], w_down[:, cols], preferred_element_type=F32)
            rows[part, :, :, :, cols] = partial.astype(BF16).reshape(4, 4, 16, quarter)

    def r_send(part, link, event, src, dst):
        pltpu.make_async_remote_copy(
            src_ref=src, dst_ref=dst,
            send_sem=reduce_send.at[part, event], recv_sem=reduce_recv.at[part, link, event],
            device_id=LINK[link], device_id_type=MESH,
        ).start()

    def r_wait(part, link, event, dst):
        pltpu.make_async_copy(dst, dst, reduce_recv.at[part, link, event]).wait()

    def add(index, *terms):
        total = rows[index].astype(F32)
        for term in terms:
            total = total + term.astype(F32)
        rows[index] = total.astype(BF16)

    def reduce_1(part):
        r_send(part, 2, 0, rows.at[part, y2, :, :, q[0]], near_y1.at[part, 0])
        r_send(part, 3, 0, rows.at[part, y2, :, :, q[1]], near_y1.at[part, 1])
        r_send(part, 0, 0, rows.at[part, :, z2, :, q[2]], near_z1.at[part, 0])
        r_send(part, 1, 0, rows.at[part, :, z2, :, q[3]], near_z1.at[part, 1])

    def reduce_2(part):
        r_wait(part, 2, 0, near_y1.at[part, 0])
        add((part, yp, ALL, slice(None), q[0]), near_y1[part, 0])
        r_send(part, 2, 1, rows.at[part, yp, :, :, a_cols], near_y2.at[part, 0])
        r_wait(part, 3, 0, near_y1.at[part, 1])
        add((part, ym, ALL, slice(None), q[1]), near_y1[part, 1])
        r_send(part, 3, 1, rows.at[part, ym, :, :, a_cols], near_y2.at[part, 1])
        r_wait(part, 0, 0, near_z1.at[part, 0])
        add((part, ALL, zp, slice(None), q[2]), near_z1[part, 0])
        r_send(part, 0, 1, rows.at[part, :, zp, :, b_cols], near_z2.at[part, 0])
        r_wait(part, 1, 0, near_z1.at[part, 1])
        add((part, ALL, zm, slice(None), q[3]), near_z1[part, 1])
        r_send(part, 1, 1, rows.at[part, :, zm, :, b_cols], near_z2.at[part, 1])

    def reduce_3(part):
        r_wait(part, 2, 1, near_y2.at[part, 0])
        r_wait(part, 3, 1, near_y2.at[part, 1])
        add((part, y, ALL, slice(None), a_cols), near_y2[part, 0], near_y2[part, 1])
        r_send(part, 0, 2, rows.at[part, y, z2, :, q[0]], far_z1.at[part, 0])
        r_send(part, 1, 2, rows.at[part, y, z2, :, q[1]], far_z1.at[part, 1])
        r_wait(part, 0, 1, near_z2.at[part, 0])
        r_wait(part, 1, 1, near_z2.at[part, 1])
        add((part, ALL, z, slice(None), b_cols), near_z2[part, 0], near_z2[part, 1])
        r_send(part, 2, 2, rows.at[part, y2, z, :, q[2]], far_y1.at[part, 0])
        r_send(part, 3, 2, rows.at[part, y2, z, :, q[3]], far_y1.at[part, 1])

    def reduce_4(part):
        r_wait(part, 0, 2, far_z1.at[part, 0])
        add((part, y, zp, slice(None), q[0]), far_z1[part, 0])
        r_send(part, 0, 3, rows.at[part, y, zp, :, a_cols], far_z2.at[part, 0])
        r_wait(part, 1, 2, far_z1.at[part, 1])
        add((part, y, zm, slice(None), q[1]), far_z1[part, 1])
        r_send(part, 1, 3, rows.at[part, y, zm, :, a_cols], far_z2.at[part, 1])
        r_wait(part, 2, 2, far_y1.at[part, 0])
        add((part, yp, z, slice(None), q[2]), far_y1[part, 0])
        r_send(part, 2, 3, rows.at[part, yp, z, :, b_cols], far_y2.at[part, 0])
        r_wait(part, 3, 2, far_y1.at[part, 1])
        add((part, ym, z, slice(None), q[3]), far_y1[part, 1])
        r_send(part, 3, 3, rows.at[part, ym, z, :, b_cols], far_y2.at[part, 1])

    def back_copy(part, to_core):
        dest = ((x + chip_offset(part)) % 4) * 2 + to_core
        return pltpu.make_async_remote_copy(
            src_ref=blocks_back.at[part, to_core], dst_ref=returned.at[att],
            send_sem=back_send.at[part, to_core], recv_sem=back_recv.at[att],
            device_id=(dest, ffn), device_id_type=MESH,
        )

    def reduce_5(part):
        for side in range(2):
            r_wait(part, side, 3, far_z2.at[part, side])
            r_wait(part, 2 + side, 3, far_y2.at[part, side])
        left = rows[part, y, z, :, a_cols].astype(F32) + far_z2[part, 0].astype(F32) + far_z2[part, 1].astype(F32)
        right = rows[part, y, z, :, b_cols].astype(F32) + far_y2[part, 0].astype(F32) + far_y2[part, 1].astype(F32)
        for to_core in range(2):
            lines = slice(8 * to_core, 8 * to_core + 8)
            blocks_back[part, to_core] = jnp.concatenate([left[lines], right[lines]], axis=0).astype(BF16)

        @pl.when(part == 0)
        def _():
            back_copy(part, 1 - core).start()
            returned[att] = blocks_back[0, core]

        @pl.when(part > 0)
        def _():
            back_copy(part, 0).start()
            back_copy(part, 1).start()

        for event, units in enumerate((4, 8, 1, 2)):
            wait_units(reduce_send.at[part, event], part, units)

    gather_own(0)
    for load in loads:
        load.wait()

    @pl.loop(0, 6)
    def _(step):
        gathering = step < 4
        computing = jnp.logical_and(step >= 1, step < 5)
        reducing = step >= 2
        at_c, at_r = step - 1, step - 2

        @pl.when(reducing)
        def _():
            reduce_2(at_r)

        @pl.when(gathering)
        def _():
            gather_a(step)

        @pl.when(computing)
        def _():
            project(at_c, 0, 2)

        @pl.when(gathering)
        def _():
            gather_b(step)

        @pl.when(computing)
        def _():
            project(at_c, 2, 4)

        @pl.when(gathering)
        def _():
            gather_c(step)

        @pl.when(step < 3)
        def _():
            gather_own(step + 1)

        @pl.when(reducing)
        def _():
            reduce_3(at_r)

        @pl.when(computing)
        def _():
            activate()
            gather_sent(at_c)
            lower_rows(at_c, 0, 2)

        @pl.when(gathering)
        def _():
            gather_d(step)

        @pl.when(reducing)
        def _():
            reduce_4(at_r)

        @pl.when(computing)
        def _():
            lower_rows(at_c, 2, 4)

        @pl.when(gathering)
        def _():
            gather_e(step)

        @pl.when(computing)
        def _():
            reduce_1(at_c)

        @pl.when(reducing)
        def _():
            reduce_5(at_r)

    in_copy(0, 1 - core).wait_send()
    back_copy(0, 1 - core).wait_send()
    for part in range(1, 4):
        for to_core in range(2):
            in_copy(part, to_core).wait_send()
            back_copy(part, to_core).wait_send()
    for step in range(1, 8):
        source = (att + step) % 8
        pltpu.make_async_copy(blocks_out.at[0], returned.at[source], back_recv.at[source]).wait()
    lines = returned[...].reshape(128, half)
    out[:, :half] = (
        hidden[:, :half].astype(F32) + jnp.dot(table_a, lines, preferred_element_type=F32)
    ).astype(BF16)
    out[:, half:] = (
        hidden[:, half:].astype(F32) + jnp.dot(table_b, lines, preferred_element_type=F32)
    ).astype(BF16)


def per_device(hidden, route, norm_gain, gate_weight, up_weight, down_weight):
    row_count, width = hidden.shape
    units = gate_weight.shape[2]
    half, quarter = width // 2, width // 4
    vmem, dma = pltpu.VMEM, pltpu.SemaphoreType.DMA
    return pl.pallas_call(
        ffn_kernel,
        out_shape=jax.ShapeDtypeStruct((row_count, width), BF16),
        in_specs=[pl.BlockSpec(memory_space=vmem)] * 3 + [pl.BlockSpec(memory_space=pl.ANY)] * 3,
        out_specs=pl.BlockSpec(memory_space=vmem),
        scratch_shapes=[
            vmem((width, units), BF16),
            vmem((width, units), BF16),
            vmem((units, width), BF16),
            vmem((8, 16, half), BF16),
            vmem((4, 2, 16, half), BF16),
            vmem((4, 2, 16, half), BF16),
            vmem((8, 16, half), BF16),
            vmem((4, 4, 4, 16, width), BF16),
            vmem((256, units), F32),
            vmem((256, units), F32),
            vmem((256, units), BF16),
            vmem((4, 2, 4, 16, quarter), BF16),
            vmem((4, 2, 4, 16, quarter), BF16),
            vmem((4, 2, 4, 16, half), BF16),
            vmem((4, 2, 4, 16, half), BF16),
            vmem((4, 2, 16, quarter), BF16),
            vmem((4, 2, 16, quarter), BF16),
            vmem((4, 2, 16, half), BF16),
            vmem((4, 2, 16, half), BF16),
            dma((3,)),
            dma((4, 2)),
            dma((4, 2)),
            dma((4, 2)),
            dma((8,)),
            dma((4, 9)),
            dma((4, 4, 9)),
            dma((4, 4)),
            dma((4, 4, 4)),
        ],
        compiler_params=pltpu.CompilerParams(
            collective_id=0, has_side_effects=True, vmem_limit_bytes=62 * 1024 * 1024
        ),
    )(hidden, route, norm_gain.reshape(1, width), gate_weight, up_weight, down_weight)


def solution(mesh):
    placed = (
        P(("att", "ffn"), None),
        P(("att", "ffn"), None),
        P(),
        P("att", None, "ffn"),
        P("att", None, "ffn"),
        P("att", "ffn", None),
    )
    return jax.shard_map(
        per_device, mesh=mesh, in_specs=placed, out_specs=P(("att", "ffn"), None), check_vma=False
    )
```

```python
import jax
import jax.numpy as jnp
from jax import lax
from jax.experimental import pallas as pl
from jax.experimental.pallas import tpu as pltpu
from jax.sharding import PartitionSpec as P

MESH = pl.DeviceIdType.MESH
F32 = jnp.float32
BF16 = jnp.bfloat16
FIRST = (((0,), (0,)), ((), ()))
LAST = (((1,), (1,)), ((), ()))


def chip_offset(part):
    return part + part // 2 - 2 * (part // 3)


def ffn_kernel(
    hidden, route, gain, gate_hbm, up_hbm, down_hbm, out,
    w_gate, w_up, w_down, blocks_out, blocks_in, blocks_back, returned, rows, gate_sum, up_sum, mid,
    near_y1, near_z1, near_y2, near_z2, far_z1, far_y1, far_z2, far_y2,
    w_sem, in_send, in_recv, back_send, back_recv, gather_send, gather_recv, reduce_send, reduce_recv,
):
    att, ffn = lax.axis_index("att"), lax.axis_index("ffn")
    x, core = att // 2, att % 2
    y, z = ffn // 4, ffn % 4
    yp, y2, ym = (y + 1) % 4, (y + 2) % 4, (y + 3) % 4
    zp, z2, zm = (z + 1) % 4, (z + 2) % 4, (z + 3) % 4
    width = hidden.shape[1]
    half, quarter = width // 2, width // 4
    a_cols, b_cols = pl.ds(0, half), pl.ds(half, half)
    q = [pl.ds(i * quarter, quarter) for i in range(4)]
    z_plus, z_minus, y_plus, y_minus = (att, y * 4 + zp), (att, y * 4 + zm), (att, yp * 4 + z), (att, ym * 4 + z)
    ALL = pl.ds(0, 4)

    barrier = pltpu.get_barrier_semaphore()
    for other in (z_plus, z_minus, y_plus, y_minus):
        pl.semaphore_signal(barrier, inc=1, device_id=other, device_id_type=MESH)
    for step in range(1, 8):
        pl.semaphore_signal(barrier, inc=1, device_id=((att + step) % 8, ffn), device_id_type=MESH)
    loads = [
        pltpu.make_async_copy(src.at[0], dst, w_sem.at[i])
        for i, (src, dst) in enumerate(((gate_hbm, w_gate), (up_hbm, w_up), (down_hbm, w_down)))
    ]
    for load in loads:
        load.start()

    widened = hidden[...].astype(F32)
    scale = lax.rsqrt(jnp.mean(widened * widened, axis=-1, keepdims=True) + 1e-06)
    normed = (widened * scale * gain[...]).astype(BF16)
    member = (lax.broadcasted_iota(jnp.int32, (8, 32), 0) == route[...]).astype(F32)
    earlier = (
        lax.broadcasted_iota(jnp.int32, (32, 32), 0) < lax.broadcasted_iota(jnp.int32, (32, 32), 1)
    ).astype(F32)
    before = jnp.dot(member, earlier, preferred_element_type=F32)
    rank = jnp.sum(before * member, axis=0, keepdims=True).astype(jnp.int32)
    place = route[...] * 16 + rank
    line = lax.broadcasted_iota(jnp.int32, (128, 32), 0)
    table_a = (line == place).astype(F32).astype(BF16)
    table_b = (line == place + 8).astype(F32).astype(BF16)
    placed = jnp.dot(table_a, normed[:, :half], preferred_element_type=F32)
    placed = placed + jnp.dot(table_b, normed[:, half:], preferred_element_type=F32)
    blocks_out[...] = placed.astype(BF16).reshape(8, 16, half)

    pl.semaphore_wait(barrier, 11)

    def in_copy(part, to_core):
        dest = ((x + 4 - chip_offset(part)) % 4) * 2 + to_core
        return pltpu.make_async_remote_copy(
            src_ref=blocks_out.at[dest], dst_ref=blocks_in.at[part, core],
            send_sem=in_send.at[part, to_core], recv_sem=in_recv.at[part, core],
            device_id=(dest, ffn), device_id_type=MESH,
        )

    in_copy(0, 1 - core).start()
    for part in range(1, 4):
        for to_core in range(2):
            in_copy(part, to_core).start()
    blocks_in[0, core] = blocks_out[att]

    def wait_in(part, from_core):
        pltpu.make_async_copy(blocks_out.at[0], blocks_in.at[part, from_core], in_recv.at[part, from_core]).wait()

    LINK = {0: z_plus, 1: z_minus, 2: y_plus, 3: y_minus}

    def g_send(part, link, event, at_y, at_z, cols):
        piece = rows.at[part, at_y, at_z, :, cols]
        pltpu.make_async_remote_copy(
            src_ref=piece, dst_ref=piece,
            send_sem=gather_send.at[part, event], recv_sem=gather_recv.at[part, link, event],
            device_id=LINK[link], device_id_type=MESH,
        ).start()

    def g_wait(part, link, event, cols):
        piece = rows.at[part, 0, 0, :, cols]
        pltpu.make_async_copy(piece, piece, gather_recv.at[part, link, event]).wait()

    whole = pl.ds(0, width)

    def gather_own(part):
        @pl.when(part == 0)
        def _():
            wait_in(0, 1 - core)

        @pl.when(part > 0)
        def _():
            wait_in(part, 0)
            wait_in(part, 1)

        first, second = blocks_in[part, 0].astype(F32), blocks_in[part, 1].astype(F32)
        rows[part, y, z, :, a_cols] = jnp.concatenate([first[:8], second[:8]], axis=0).astype(BF16)
        rows[part, y, z, :, b_cols] = jnp.concatenate([first[8:], second[8:]], axis=0).astype(BF16)
        for link in range(4):
            g_send(part, link, 0, y, z, whole)

    def gather_a(part):
        for link in range(4):
            g_wait(part, link, 0, whole)
        g_send(part, 0, 1, y, zm, q[0])
        g_send(part, 1, 1, y, zp, q[1])
        g_send(part, 2, 1, ym, z, q[2])
        g_send(part, 3, 1, yp, z, q[3])
        for link in (2, 3):
            g_send(part, link, 2, y, zm, a_cols)
        for link in (0, 1):
            g_send(part, link, 2, ym, z, b_cols)
        for link in (2, 3):
            g_send(part, link, 3, y, zp, a_cols)
        for link in (0, 1):
            g_send(part, link, 3, yp, z, b_cols)
        g_send(part, 0, 5, y, zm, q[2])
        g_send(part, 1, 5, y, zp, q[3])
        g_send(part, 2, 5, ym, z, q[0])
        g_send(part, 3, 5, yp, z, q[1])

    def gather_b(part):
        for link in range(4):
            g_wait(part, link, 1, q[0])
        for link in (2, 3):
            g_send(part, link, 4, y, z2, a_cols)
        for link in (0, 1):
            g_send(part, link, 4, y2, z, b_cols)

    def gather_on(part, event, of_y, of_z):
        for link in range(4):
            g_wait(part, link, event, a_cols)
        g_send(part, 0, event + 4, of_y, zm, q[2])
        g_send(part, 1, event + 4, of_y, zp, q[3])
        g_send(part, 2, event + 4, ym, of_z, q[0])
        g_send(part, 3, event + 4, yp, of_z, q[1])

    def gather_c(part):
        gather_on(part, 2, ym, zm)
        gather_on(part, 3, yp, zp)

    def gather_d(part):
        gather_on(part, 4, y2, z2)

    def gather_e(part):
        for event in range(5, 9):
            for link in range(4):
                g_wait(part, link, event, q[0])

    def wait_units(sem, part, units):
        piece = rows.at[part, 0, pl.ds(0, units)] if units <= 4 else rows.at[part, pl.ds(0, units // 4)]
        pltpu.make_async_copy(piece, piece, sem).wait()

    def gather_sent(part):
        for event, units in enumerate((4, 1, 2, 2, 2, 1, 1, 1, 1)):
            wait_units(gather_send.at[part, event], part, units)

    def project(part, lower, upper):
        @pl.loop(lower, upper)
        def _(i):
            cols = pl.ds(pl.multiple_of(i * quarter, quarter), quarter)
            block = rows[part, :, :, :, cols].reshape(256, quarter)
            gate = lax.dot_general(block, w_gate[:, cols], LAST, preferred_element_type=F32)
            up = lax.dot_general(block, w_up[:, cols], LAST, preferred_element_type=F32)

            @pl.when(i == 0)
            def _():
                gate_sum[...] = gate
                up_sum[...] = up

            @pl.when(i > 0)
            def _():
                gate_sum[...] += gate
                up_sum[...] += up

    def activate():
        gate = gate_sum[...]
        mid[...] = (gate / (1.0 + jnp.exp(-gate)) * up_sum[...]).astype(BF16)

    def lower_rows(part, lower, upper):
        @pl.loop(lower, upper)
        def _(i):
            cols = pl.ds(pl.multiple_of(i * quarter, quarter), quarter)
            partial = jnp.dot(mid[...], w_down[:, cols], preferred_element_type=F32)
            rows[part, :, :, :, cols] = partial.astype(BF16).reshape(4, 4, 16, quarter)

    def r_send(part, link, event, src, dst):
        pltpu.make_async_remote_copy(
            src_ref=src, dst_ref=dst,
            send_sem=reduce_send.at[part, event], recv_sem=reduce_recv.at[part, link, event],
            device_id=LINK[link], device_id_type=MESH,
        ).start()

    def r_wait(part, link, event, dst):
        pltpu.make_async_copy(dst, dst, reduce_recv.at[part, link, event]).wait()

    def add(index, *terms):
        total = rows[index].astype(F32)
        for term in terms:
            total = total + term.astype(F32)
        rows[index] = total.astype(BF16)

    def reduce_1(part):
        r_send(part, 2, 0, rows.at[part, y2, :, :, q[0]], near_y1.at[part, 0])
        r_send(part, 3, 0, rows.at[part, y2, :, :, q[1]], near_y1.at[part, 1])
        r_send(part, 0, 0, rows.at[part, :, z2, :, q[2]], near_z1.at[part, 0])
        r_send(part, 1, 0, rows.at[part, :, z2, :, q[3]], near_z1.at[part, 1])

    def reduce_2(part):
        r_wait(part, 2, 0, near_y1.at[part, 0])
        add((part, yp, ALL, slice(None), q[0]), near_y1[part, 0])
        r_send(part, 2, 1, rows.at[part, yp, :, :, a_cols], near_y2.at[part, 0])
        r_wait(part, 3, 0, near_y1.at[part, 1])
        add((part, ym, ALL, slice(None), q[1]), near_y1[part, 1])
        r_send(part, 3, 1, rows.at[part, ym, :, :, a_cols], near_y2.at[part, 1])
        r_wait(part, 0, 0, near_z1.at[part, 0])
        add((part, ALL, zp, slice(None), q[2]), near_z1[part, 0])
        r_send(part, 0, 1, rows.at[part, :, zp, :, b_cols], near_z2.at[part, 0])
        r_wait(part, 1, 0, near_z1.at[part, 1])
        add((part, ALL, zm, slice(None), q[3]), near_z1[part, 1])
        r_send(part, 1, 1, rows.at[part, :, zm, :, b_cols], near_z2.at[part, 1])

    def reduce_3(part):
        r_wait(part, 2, 1, near_y2.at[part, 0])
        r_wait(part, 3, 1, near_y2.at[part, 1])
        add((part, y, ALL, slice(None), a_cols), near_y2[part, 0], near_y2[part, 1])
        r_send(part, 0, 2, rows.at[part, y, z2, :, q[0]], far_z1.at[part, 0])
        r_send(part, 1, 2, rows.at[part, y, z2, :, q[1]], far_z1.at[part, 1])
        r_wait(part, 0, 1, near_z2.at[part, 0])
        r_wait(part, 1, 1, near_z2.at[part, 1])
        add((part, ALL, z, slice(None), b_cols), near_z2[part, 0], near_z2[part, 1])
        r_send(part, 2, 2, rows.at[part, y2, z, :, q[2]], far_y1.at[part, 0])
        r_send(part, 3, 2, rows.at[part, y2, z, :, q[3]], far_y1.at[part, 1])

    def reduce_4(part):
        r_wait(part, 0, 2, far_z1.at[part, 0])
        add((part, y, zp, slice(None), q[0]), far_z1[part, 0])
        r_send(part, 0, 3, rows.at[part, y, zp, :, a_cols], far_z2.at[part, 0])
        r_wait(part, 1, 2, far_z1.at[part, 1])
        add((part, y, zm, slice(None), q[1]), far_z1[part, 1])
        r_send(part, 1, 3, rows.at[part, y, zm, :, a_cols], far_z2.at[part, 1])
        r_wait(part, 2, 2, far_y1.at[part, 0])
        add((part, yp, z, slice(None), q[2]), far_y1[part, 0])
        r_send(part, 2, 3, rows.at[part, yp, z, :, b_cols], far_y2.at[part, 0])
        r_wait(part, 3, 2, far_y1.at[part, 1])
        add((part, ym, z, slice(None), q[3]), far_y1[part, 1])
        r_send(part, 3, 3, rows.at[part, ym, z, :, b_cols], far_y2.at[part, 1])

    def back_copy(part, to_core):
        dest = ((x + chip_offset(part)) % 4) * 2 + to_core
        return pltpu.make_async_remote_copy(
            src_ref=blocks_back.at[part, to_core], dst_ref=returned.at[att],
            send_sem=back_send.at[part, to_core], recv_sem=back_recv.at[att],
            device_id=(dest, ffn), device_id_type=MESH,
        )

    def reduce_5(part):
        for side in range(2):
            r_wait(part, side, 3, far_z2.at[part, side])
            r_wait(part, 2 + side, 3, far_y2.at[part, side])
        left = rows[part, y, z, :, a_cols].astype(F32) + far_z2[part, 0].astype(F32) + far_z2[part, 1].astype(F32)
        right = rows[part, y, z, :, b_cols].astype(F32) + far_y2[part, 0].astype(F32) + far_y2[part, 1].astype(F32)
        for to_core in range(2):
            lines = slice(8 * to_core, 8 * to_core + 8)
            blocks_back[part, to_core] = jnp.concatenate([left[lines], right[lines]], axis=0).astype(BF16)

        @pl.when(part == 0)
        def _():
            back_copy(part, 1 - core).start()
            returned[att] = blocks_back[0, core]

        @pl.when(part > 0)
        def _():
            back_copy(part, 0).start()
            back_copy(part, 1).start()

        for event, units in enumerate((4, 8, 1, 2)):
            wait_units(reduce_send.at[part, event], part, units)

    gather_own(0)

    @pl.loop(0, 6)
    def _(step):
        gathering = step < 4
        computing = jnp.logical_and(step >= 1, step < 5)
        reducing = step >= 2
        at_c, at_r = step - 1, step - 2

        @pl.when(reducing)
        def _():
            reduce_2(at_r)

        @pl.when(gathering)
        def _():
            gather_a(step)

        @pl.when(step == 1)
        def _():
            for load in loads:
                load.wait()

        @pl.when(computing)
        def _():
            project(at_c, 0, 2)

        @pl.when(gathering)
        def _():
            gather_b(step)

        @pl.when(computing)
        def _():
            project(at_c, 2, 4)

        @pl.when(gathering)
        def _():
            gather_c(step)

        @pl.when(step < 3)
        def _():
            gather_own(step + 1)

        @pl.when(reducing)
        def _():
            reduce_3(at_r)

        @pl.when(computing)
        def _():
            activate()
            gather_sent(at_c)
            lower_rows(at_c, 0, 2)

        @pl.when(gathering)
        def _():
            gather_d(step)

        @pl.when(reducing)
        def _():
            reduce_4(at_r)

        @pl.when(computing)
        def _():
            lower_rows(at_c, 2, 4)

        @pl.when(gathering)
        def _():
            gather_e(step)

        @pl.when(computing)
        def _():
            reduce_1(at_c)

        @pl.when(reducing)
        def _():
            reduce_5(at_r)

    in_copy(0, 1 - core).wait_send()
    back_copy(0, 1 - core).wait_send()
    for part in range(1, 4):
        for to_core in range(2):
            in_copy(part, to_core).wait_send()
            back_copy(part, to_core).wait_send()
    for step in range(1, 8):
        source = (att + step) % 8
        pltpu.make_async_copy(blocks_out.at[0], returned.at[source], back_recv.at[source]).wait()
    lines = returned[...].reshape(128, half)
    out[:, :half] = (
        hidden[:, :half].astype(F32) + lax.dot_general(table_a, lines, FIRST, preferred_element_type=F32)
    ).astype(BF16)
    out[:, half:] = (
        hidden[:, half:].astype(F32) + lax.dot_general(table_b, lines, FIRST, preferred_element_type=F32)
    ).astype(BF16)


def per_device(hidden, route, norm_gain, gate_weight, up_weight, down_weight):
    row_count, width = hidden.shape
    units = gate_weight.shape[2]
    half, quarter = width // 2, width // 4
    vmem, dma = pltpu.VMEM, pltpu.SemaphoreType.DMA
    return pl.pallas_call(
        ffn_kernel,
        out_shape=jax.ShapeDtypeStruct((row_count, width), BF16),
        in_specs=[pl.BlockSpec(memory_space=vmem)] * 3 + [pl.BlockSpec(memory_space=pl.ANY)] * 3,
        out_specs=pl.BlockSpec(memory_space=vmem),
        scratch_shapes=[
            vmem((units, width), BF16),
            vmem((units, width), BF16),
            vmem((units, width), BF16),
            vmem((8, 16, half), BF16),
            vmem((4, 2, 16, half), BF16),
            vmem((4, 2, 16, half), BF16),
            vmem((8, 16, half), BF16),
            vmem((4, 4, 4, 16, width), BF16),
            vmem((256, units), F32),
            vmem((256, units), F32),
            vmem((256, units), BF16),
            vmem((4, 2, 4, 16, quarter), BF16),
            vmem((4, 2, 4, 16, quarter), BF16),
            vmem((4, 2, 4, 16, half), BF16),
            vmem((4, 2, 4, 16, half), BF16),
            vmem((4, 2, 16, quarter), BF16),
            vmem((4, 2, 16, quarter), BF16),
            vmem((4, 2, 16, half), BF16),
            vmem((4, 2, 16, half), BF16),
            dma((3,)),
            dma((4, 2)),
            dma((4, 2)),
            dma((4, 2)),
            dma((8,)),
            dma((4, 9)),
            dma((4, 4, 9)),
            dma((4, 4)),
            dma((4, 4, 4)),
        ],
        compiler_params=pltpu.CompilerParams(
            collective_id=0, has_side_effects=True, vmem_limit_bytes=62 * 1024 * 1024
        ),
    )(
        hidden, route.reshape(1, row_count), norm_gain.reshape(1, width),
        jnp.swapaxes(gate_weight, 1, 2), jnp.swapaxes(up_weight, 1, 2), down_weight,
    )


def solution(mesh):
    placed = (
        P(("att", "ffn"), None),
        P(("att", "ffn"), None),
        P(),
        P("att", None, "ffn"),
        P("att", None, "ffn"),
        P("att", "ffn", None),
    )
    return jax.shard_map(
        per_device, mesh=mesh, in_specs=placed, out_specs=P(("att", "ffn"), None), check_vma=False
    )
```

```python
import jax
import jax.numpy as jnp
from jax import lax
from jax.experimental import pallas as pl
from jax.experimental.pallas import tpu as pltpu
from jax.sharding import PartitionSpec as P

MESH = pl.DeviceIdType.MESH
F32 = jnp.float32
BF16 = jnp.bfloat16
FIRST = (((0,), (0,)), ((), ()))
LAST = (((1,), (1,)), ((), ()))


def ffn_kernel(
    hidden, route, gain, gate_hbm, up_hbm, down_hbm, out,
    w_gate, w_up, w_down, blocks_out, blocks_in, blocks_back, returned, rows, gate_sum, up_sum, mid,
    near_y1, near_z1, near_y2, near_z2, far_z1, far_y1, far_z2, far_y2,
    w_sem, in_send, in_recv, back_send, back_recv, gather_send, gather_recv, reduce_send, reduce_recv,
):
    att, ffn = lax.axis_index("att"), lax.axis_index("ffn")
    x, core = att // 2, att % 2
    y, z = ffn // 4, ffn % 4
    yp, y2, ym = (y + 1) % 4, (y + 2) % 4, (y + 3) % 4
    zp, z2, zm = (z + 1) % 4, (z + 2) % 4, (z + 3) % 4
    width = hidden.shape[1]
    half, quarter = width // 2, width // 4
    a_cols, b_cols = pl.ds(0, half), pl.ds(half, half)
    q = [pl.ds(i * quarter, quarter) for i in range(4)]
    z_plus, z_minus, y_plus, y_minus = (att, y * 4 + zp), (att, y * 4 + zm), (att, yp * 4 + z), (att, ym * 4 + z)
    ALL = pl.ds(0, 4)

    barrier = pltpu.get_barrier_semaphore()
    for other in (z_plus, z_minus, y_plus, y_minus):
        pl.semaphore_signal(barrier, inc=1, device_id=other, device_id_type=MESH)
    for step in range(1, 8):
        pl.semaphore_signal(barrier, inc=1, device_id=((att + step) % 8, ffn), device_id_type=MESH)
    loads = [
        pltpu.make_async_copy(src.at[0], dst, w_sem.at[i])
        for i, (src, dst) in enumerate(((gate_hbm, w_gate), (up_hbm, w_up), (down_hbm, w_down)))
    ]
    for load in loads:
        load.start()

    widened = hidden[...].astype(F32)
    scale = lax.rsqrt(jnp.mean(widened * widened, axis=-1, keepdims=True) + 1e-06)
    normed = (widened * scale * gain[...]).astype(BF16)
    member = (lax.broadcasted_iota(jnp.int32, (8, 32), 0) == route[...]).astype(F32)
    earlier = (
        lax.broadcasted_iota(jnp.int32, (32, 32), 0) < lax.broadcasted_iota(jnp.int32, (32, 32), 1)
    ).astype(F32)
    before = jnp.dot(member, earlier, preferred_element_type=F32)
    rank = jnp.sum(before * member, axis=0, keepdims=True).astype(jnp.int32)
    place = route[...] * 16 + rank
    line = lax.broadcasted_iota(jnp.int32, (128, 32), 0)
    table_a = (line == place).astype(F32).astype(BF16)
    table_b = (line == place + 8).astype(F32).astype(BF16)
    placed = jnp.dot(table_a, normed[:, :half], preferred_element_type=F32)
    placed = placed + jnp.dot(table_b, normed[:, half:], preferred_element_type=F32)
    blocks_out[...] = placed.astype(BF16).reshape(8, 16, half)

    pl.semaphore_wait(barrier, 11)

    def in_copy(part, to_core):
        dest = ((x + 4 - part) % 4) * 2 + to_core
        return pltpu.make_async_remote_copy(
            src_ref=blocks_out.at[dest], dst_ref=blocks_in.at[part, core],
            send_sem=in_send.at[part, to_core], recv_sem=in_recv.at[part, core],
            device_id=(dest, ffn), device_id_type=MESH,
        )

    in_copy(0, 1 - core).start()
    for part in range(1, 4):
        for to_core in range(2):
            in_copy(part, to_core).start()
    blocks_in[0, core] = blocks_out[att]

    def wait_in(part, from_core):
        pltpu.make_async_copy(blocks_out.at[0], blocks_in.at[part, from_core], in_recv.at[part, from_core]).wait()

    LINK = {0: z_plus, 1: z_minus, 2: y_plus, 3: y_minus}

    def g_send(part, link, event, at_y, at_z, cols):
        piece = rows.at[part, at_y, at_z, :, cols]
        pltpu.make_async_remote_copy(
            src_ref=piece, dst_ref=piece,
            send_sem=gather_send.at[part, event], recv_sem=gather_recv.at[part, link, event],
            device_id=LINK[link], device_id_type=MESH,
        ).start()

    def g_wait(part, link, event, cols):
        piece = rows.at[part, 0, 0, :, cols]
        pltpu.make_async_copy(piece, piece, gather_recv.at[part, link, event]).wait()

    whole = pl.ds(0, width)

    def gather_own(part):
        @pl.when(part == 0)
        def _():
            wait_in(0, 1 - core)

        @pl.when(part > 0)
        def _():
            wait_in(part, 0)
            wait_in(part, 1)

        first, second = blocks_in[part, 0].astype(F32), blocks_in[part, 1].astype(F32)
        rows[part, y, z, :, a_cols] = jnp.concatenate([first[:8], second[:8]], axis=0).astype(BF16)
        rows[part, y, z, :, b_cols] = jnp.concatenate([first[8:], second[8:]], axis=0).astype(BF16)
        for link in range(4):
            g_send(part, link, 0, y, z, whole)

    def gather_a(part):
        for link in range(4):
            g_wait(part, link, 0, whole)
        g_send(part, 0, 1, y, zm, q[0])
        g_send(part, 1, 1, y, zp, q[1])
        g_send(part, 2, 1, ym, z, q[2])
        g_send(part, 3, 1, yp, z, q[3])
        for link in (2, 3):
            g_send(part, link, 2, y, zm, a_cols)
        for link in (0, 1):
            g_send(part, link, 2, ym, z, b_cols)
        for link in (2, 3):
            g_send(part, link, 3, y, zp, a_cols)
        for link in (0, 1):
            g_send(part, link, 3, yp, z, b_cols)
        g_send(part, 0, 5, y, zm, q[2])
        g_send(part, 1, 5, y, zp, q[3])
        g_send(part, 2, 5, ym, z, q[0])
        g_send(part, 3, 5, yp, z, q[1])

    def gather_b(part):
        for link in range(4):
            g_wait(part, link, 1, q[0])
        for link in (2, 3):
            g_send(part, link, 4, y, z2, a_cols)
        for link in (0, 1):
            g_send(part, link, 4, y2, z, b_cols)

    def gather_on(part, event, of_y, of_z):
        for link in range(4):
            g_wait(part, link, event, a_cols)
        g_send(part, 0, event + 4, of_y, zm, q[2])
        g_send(part, 1, event + 4, of_y, zp, q[3])
        g_send(part, 2, event + 4, ym, of_z, q[0])
        g_send(part, 3, event + 4, yp, of_z, q[1])

    def gather_c(part):
        gather_on(part, 2, ym, zm)
        gather_on(part, 3, yp, zp)

    def gather_d(part):
        gather_on(part, 4, y2, z2)

    def gather_e(part):
        for event in range(5, 9):
            for link in range(4):
                g_wait(part, link, event, q[0])

    def wait_units(sem, part, units):
        piece = rows.at[part, 0, pl.ds(0, units)] if units <= 4 else rows.at[part, pl.ds(0, units // 4)]
        pltpu.make_async_copy(piece, piece, sem).wait()

    def gather_sent(part):
        for event, units in enumerate((4, 1, 2, 2, 2, 1, 1, 1, 1)):
            wait_units(gather_send.at[part, event], part, units)

    def project(part, lower, upper):
        @pl.loop(lower, upper)
        def _(i):
            cols = pl.ds(pl.multiple_of(i * quarter, quarter), quarter)
            block = rows[part, :, :, :, cols].reshape(256, quarter)
            gate = lax.dot_general(w_gate[:, cols], block, LAST, preferred_element_type=F32)
            up = lax.dot_general(w_up[:, cols], block, LAST, preferred_element_type=F32)

            @pl.when(i == 0)
            def _():
                gate_sum[...] = gate
                up_sum[...] = up

            @pl.when(i > 0)
            def _():
                gate_sum[...] += gate
                up_sum[...] += up

    def activate():
        gate = gate_sum[...]
        mid[...] = (gate / (1.0 + jnp.exp(-gate)) * up_sum[...]).T.astype(BF16)

    def lower_rows(part, lower, upper):
        @pl.loop(lower, upper)
        def _(i):
            cols = pl.ds(pl.multiple_of(i * quarter, quarter), quarter)
            partial = jnp.dot(mid[...], w_down[:, cols], preferred_element_type=F32)
            rows[part, :, :, :, cols] = partial.astype(BF16).reshape(4, 4, 16, quarter)

    def r_send(part, link, event, src, dst):
        pltpu.make_async_remote_copy(
            src_ref=src, dst_ref=dst,
            send_sem=reduce_send.at[part, 3 if event == 9 else event // 4], recv_sem=reduce_recv.at[part, link, event],
            device_id=LINK[link], device_id_type=MESH,
        ).start()

    def r_wait(part, link, event, dst):
        pltpu.make_async_copy(dst, dst, reduce_recv.at[part, link, event]).wait()

    def add(index, *terms):
        total = rows[index].astype(F32)
        for term in terms:
            total = total + term.astype(F32)
        rows[index] = total.astype(BF16)

    across_z, across_y = (z2, zp, zm, z), (y2, yp, ym, y)

    def reduce_1a(part):
        for i in range(4):
            r_send(part, 2, i, rows.at[part, y2, across_z[i], :, q[0]], near_y1.at[part, 0, i])
            r_send(part, 3, i, rows.at[part, y2, across_z[i], :, q[1]], near_y1.at[part, 1, i])

    def reduce_1b(part):
        for i in range(4):
            r_send(part, 0, i, rows.at[part, across_y[i], z2, :, q[2]], near_z1.at[part, 0, i])
            r_send(part, 1, i, rows.at[part, across_y[i], z2, :, q[3]], near_z1.at[part, 1, i])

    def reduce_2(part):
        for i in range(4):
            at_y, at_z = across_y[i], across_z[i]
            for side, goal in ((0, yp), (1, ym)):
                r_wait(part, 2 + side, i, near_y1.at[part, side, i])
                add((part, goal, at_z, slice(None), q[side]), near_y1[part, side, i])
                r_send(part, 2 + side, 4 + i, rows.at[part, goal, at_z, :, a_cols], near_y2.at[part, side, i])
            for side, goal in ((0, zp), (1, zm)):
                r_wait(part, side, i, near_z1.at[part, side, i])
                add((part, at_y, goal, slice(None), q[2 + side]), near_z1[part, side, i])
                r_send(part, side, 4 + i, rows.at[part, at_y, goal, :, b_cols], near_z2.at[part, side, i])

    def reduce_3(part, pieces):
        for i in pieces:
            at_y, at_z = across_y[i], across_z[i]
            r_wait(part, 2, 4 + i, near_y2.at[part, 0, i])
            r_wait(part, 3, 4 + i, near_y2.at[part, 1, i])
            add((part, y, at_z, slice(None), a_cols), near_y2[part, 0, i], near_y2[part, 1, i])
            r_wait(part, 0, 4 + i, near_z2.at[part, 0, i])
            r_wait(part, 1, 4 + i, near_z2.at[part, 1, i])
            add((part, at_y, z, slice(None), b_cols), near_z2[part, 0, i], near_z2[part, 1, i])
            if i == 0:
                for side in range(2):
                    r_send(part, side, 8, rows.at[part, y, z2, :, q[side]], far_z1.at[part, side])
                    r_send(part, 2 + side, 8, rows.at[part, y2, z, :, q[2 + side]], far_y1.at[part, side])
            elif i < 3:
                side = i - 1
                r_wait(part, side, 8, far_z1.at[part, side])
                add((part, y, at_z, slice(None), q[side]), far_z1[part, side])
                r_send(part, side, 9, rows.at[part, y, at_z, :, a_cols], far_z2.at[part, side])
                r_wait(part, 2 + side, 8, far_y1.at[part, side])
                add((part, at_y, z, slice(None), q[2 + side]), far_y1[part, side])
                r_send(part, 2 + side, 9, rows.at[part, at_y, z, :, b_cols], far_y2.at[part, side])

    def back_copy(part, to_core):
        dest = ((x + part) % 4) * 2 + to_core
        return pltpu.make_async_remote_copy(
            src_ref=blocks_back.at[part, to_core], dst_ref=returned.at[att],
            send_sem=back_send.at[part, to_core], recv_sem=back_recv.at[att],
            device_id=(dest, ffn), device_id_type=MESH,
        )

    def reduce_5(part):
        for side in range(2):
            r_wait(part, side, 9, far_z2.at[part, side])
            r_wait(part, 2 + side, 9, far_y2.at[part, side])
        left = rows[part, y, z, :, a_cols].astype(F32) + far_z2[part, 0].astype(F32) + far_z2[part, 1].astype(F32)
        right = rows[part, y, z, :, b_cols].astype(F32) + far_y2[part, 0].astype(F32) + far_y2[part, 1].astype(F32)
        for to_core in range(2):
            lines = slice(8 * to_core, 8 * to_core + 8)
            blocks_back[part, to_core] = jnp.concatenate([left[lines], right[lines]], axis=0).astype(BF16)

        if isinstance(part, int) and part == 0:
            back_copy(part, 1 - core).start()
            returned[att] = blocks_back[part, core]
        else:
            back_copy(part, 0).start()
            back_copy(part, 1).start()

        for event, units in enumerate((4, 8, 1, 2)):
            wait_units(reduce_send.at[part, event], part, units)

    gather_own(0)
    gather_own(1)

    @pl.loop(0, 6)
    def _(step):
        gathering = step < 4
        computing = jnp.logical_and(step >= 1, step < 5)
        sending = jnp.logical_and(step >= 2, step < 5)
        reducing = step >= 3
        at_c, at_r = step - 1, step - 2

        @pl.when(gathering)
        def _():
            gather_a(step)

        @pl.when(reducing)
        def _():
            reduce_2(at_r % 3)

        @pl.when(step == 4)
        def _():
            reduce_1a(0)
            reduce_1b(0)

        @pl.when(step >= 4)
        def _():
            reduce_5(step - 3)

        @pl.when(computing)
        def _():
            gather_e(at_c)

        @pl.when(step == 1)
        def _():
            for load in loads:
                load.wait()

        @pl.when(computing)
        def _():
            project(at_c, 0, 2)

        @pl.when(gathering)
        def _():
            gather_b(step)

        @pl.when(computing)
        def _():
            project(at_c, 2, 4)

        @pl.when(gathering)
        def _():
            gather_c(step)

        @pl.when(step < 2)
        def _():
            gather_own(step + 2)

        @pl.when(computing)
        def _():
            activate()
            gather_sent(at_c)
            lower_rows(at_c, 0, 2)

        @pl.when(sending)
        def _():
            reduce_1a(at_c)

        @pl.when(gathering)
        def _():
            gather_d(step)

        @pl.when(computing)
        def _():
            lower_rows(at_c, 2, 4)

        @pl.when(sending)
        def _():
            reduce_1b(at_c)

        @pl.when(reducing)
        def _():
            reduce_3(at_r, (0,))

        @pl.when(step == 4)
        def _():
            reduce_2(3)

        @pl.when(reducing)
        def _():
            reduce_3(at_r, (1, 2, 3))

        @pl.when(step == 5)
        def _():
            reduce_3(0, (0,))

    reduce_3(0, (1, 2, 3))
    reduce_5(3)
    reduce_5(0)
    in_copy(0, 1 - core).wait_send()
    back_copy(0, 1 - core).wait_send()
    for part in range(1, 4):
        for to_core in range(2):
            in_copy(part, to_core).wait_send()
            back_copy(part, to_core).wait_send()
    for step in range(1, 8):
        source = (att + step) % 8
        pltpu.make_async_copy(blocks_out.at[0], returned.at[source], back_recv.at[source]).wait()
    lines = returned[...].reshape(128, half)
    out[:, :half] = (
        hidden[:, :half].astype(F32) + lax.dot_general(table_a, lines, FIRST, preferred_element_type=F32)
    ).astype(BF16)
    out[:, half:] = (
        hidden[:, half:].astype(F32) + lax.dot_general(table_b, lines, FIRST, preferred_element_type=F32)
    ).astype(BF16)


def per_device(hidden, route, norm_gain, gate_weight, up_weight, down_weight):
    row_count, width = hidden.shape
    units = gate_weight.shape[2]
    half, quarter = width // 2, width // 4
    vmem, dma = pltpu.VMEM, pltpu.SemaphoreType.DMA
    return pl.pallas_call(
        ffn_kernel,
        out_shape=jax.ShapeDtypeStruct((row_count, width), BF16),
        in_specs=[pl.BlockSpec(memory_space=vmem)] * 3 + [pl.BlockSpec(memory_space=pl.ANY)] * 3,
        out_specs=pl.BlockSpec(memory_space=vmem),
        scratch_shapes=[
            vmem((units, width), BF16),
            vmem((units, width), BF16),
            vmem((units, width), BF16),
            vmem((8, 16, half), BF16),
            vmem((4, 2, 16, half), BF16),
            vmem((4, 2, 16, half), BF16),
            vmem((8, 16, half), BF16),
            vmem((4, 4, 4, 16, width), BF16),
            vmem((units, 256), F32),
            vmem((units, 256), F32),
            vmem((256, units), BF16),
            vmem((4, 2, 4, 16, quarter), BF16),
            vmem((4, 2, 4, 16, quarter), BF16),
            vmem((4, 2, 4, 16, half), BF16),
            vmem((4, 2, 4, 16, half), BF16),
            vmem((4, 2, 16, quarter), BF16),
            vmem((4, 2, 16, quarter), BF16),
            vmem((4, 2, 16, half), BF16),
            vmem((4, 2, 16, half), BF16),
            dma((3,)),
            dma((4, 2)),
            dma((4, 2)),
            dma((4, 2)),
            dma((8,)),
            dma((4, 9)),
            dma((4, 4, 9)),
            dma((4, 4)),
            dma((4, 4, 10)),
        ],
        compiler_params=pltpu.CompilerParams(
            collective_id=0, has_side_effects=True, vmem_limit_bytes=62 * 1024 * 1024
        ),
    )(
        hidden, route.reshape(1, row_count), norm_gain.reshape(1, width),
        jnp.swapaxes(gate_weight, 1, 2), jnp.swapaxes(up_weight, 1, 2), down_weight,
    )


def solution(mesh):
    placed = (
        P(("att", "ffn"), None),
        P(("att", "ffn"), None),
        P(),
        P("att", None, "ffn"),
        P("att", None, "ffn"),
        P("att", "ffn", None),
    )
    return jax.shard_map(
        per_device, mesh=mesh, in_specs=placed, out_specs=P(("att", "ffn"), None), check_vma=False
    )
```

```python
import jax
import jax.numpy as jnp
from jax import lax
from jax.experimental import pallas as pl
from jax.experimental.pallas import tpu as pltpu
from jax.sharding import PartitionSpec as P

MESH = pl.DeviceIdType.MESH
F32 = jnp.float32
BF16 = jnp.bfloat16
FIRST = (((0,), (0,)), ((), ()))
LAST = (((1,), (1,)), ((), ()))


RAW = 4


def chip_offset(part):
    return part + part // 2 - 2 * (part // 3)


def raw_columns(width):
    return width // 4


def halves(width):
    half = width // 2
    more = (half // 128 + 1) // 2 * 128
    less = half - more
    quarters = [pl.ds(0, more), pl.ds(more, less), pl.ds(half, less), pl.ds(half + less, more)]
    return pl.ds(0, width), pl.ds(0, half), pl.ds(half, half), quarters


def ffn_kernel(
    hidden, route, gain, gate_hbm, up_hbm, down_hbm, out,
    w_gate, w_up, w_down, blocks_out, blocks_in, blocks_back, returned, rows, raw, slots,
    gate_sum, up_sum, mid,
    near_y1, near_z1, near_y2, near_z2, far_z1, far_y1, far_z2, far_y2,
    w_sem, in_send, in_recv, shift_send, shift_recv, home_sem, back_send, back_recv, gather_send, gather_recv, reduce_send, reduce_recv,
):
    att, ffn = lax.axis_index("att"), lax.axis_index("ffn")
    x, core = att // 2, att % 2
    y, z = ffn // 4, ffn % 4
    yp, y2, ym = (y + 1) % 4, (y + 2) % 4, (y + 3) % 4
    zp, z2, zm = (z + 1) % 4, (z + 2) % 4, (z + 3) % 4
    width = hidden.shape[1]
    half, quarter = width // 2, width // 4
    a_cols, b_cols = pl.ds(0, half), pl.ds(half, half)
    q = [pl.ds(i * quarter, quarter) for i in range(4)]
    extra = raw_columns(width)
    split = width - extra
    g_half, x_half = split // 2, extra // 2
    slot_geometry, raw_geometry = halves(split), halves(2 * extra + 256)
    z_plus, z_minus, y_plus, y_minus = (att, y * 4 + zp), (att, y * 4 + zm), (att, yp * 4 + z), (att, ym * 4 + z)
    ALL = pl.ds(0, 4)

    barrier = pltpu.get_barrier_semaphore()
    for other in (z_plus, z_minus, y_plus, y_minus):
        pl.semaphore_signal(barrier, inc=1, device_id=other, device_id_type=MESH)
    for step in range(1, 8):
        pl.semaphore_signal(barrier, inc=1, device_id=((att + step) % 8, ffn), device_id_type=MESH)
    loads = [
        pltpu.make_async_copy(src.at[0], dst, w_sem.at[i])
        for i, (src, dst) in enumerate(((gate_hbm, w_gate), (up_hbm, w_up), (down_hbm, w_down)))
    ]
    for load in loads:
        load.start()

    widened = hidden[...].astype(F32)
    scale = lax.rsqrt(jnp.mean(widened * widened, axis=-1, keepdims=True) + 1e-06)
    normed = (widened * scale * gain[...]).astype(BF16)
    member = (lax.broadcasted_iota(jnp.int32, (8, 32), 0) == route[...]).astype(F32)
    earlier = (
        lax.broadcasted_iota(jnp.int32, (32, 32), 0) < lax.broadcasted_iota(jnp.int32, (32, 32), 1)
    ).astype(F32)
    before = jnp.dot(member, earlier, preferred_element_type=F32)
    rank = jnp.sum(before * member, axis=0, keepdims=True).astype(jnp.int32)
    place = route[...] * 16 + rank
    line = lax.broadcasted_iota(jnp.int32, (128, 32), 0)
    table_a = (line == place).astype(F32).astype(BF16)
    table_b = (line == place + 8).astype(F32).astype(BF16)
    placed = jnp.dot(table_a, normed[:, :g_half], preferred_element_type=F32)
    placed = placed + jnp.dot(table_b, normed[:, g_half:split], preferred_element_type=F32)
    blocks_out[...] = placed.astype(BF16).reshape(8, 16, g_half)
    number = jnp.broadcast_to(place.astype(F32), (128, 32)).T.astype(BF16)
    for i in range(2):
        lines = slice(16 * i, 16 * i + 16)
        raw[y, z, :, extra * i : extra * (i + 1)] = normed[lines, split:]
        raw[y, z, :, 2 * extra + 128 * i : 2 * extra + 128 * (i + 1)] = number[lines]

    pl.semaphore_wait(barrier, 11)

    def in_copy(part, to_core):
        dest = ((x + 4 - chip_offset(part)) % 4) * 2 + to_core
        return pltpu.make_async_remote_copy(
            src_ref=blocks_out.at[dest], dst_ref=blocks_in.at[part, core],
            send_sem=in_send.at[part, to_core], recv_sem=in_recv.at[part, core],
            device_id=(dest, ffn), device_id_type=MESH,
        )

    def wait_in(part, from_core):
        pltpu.make_async_copy(blocks_out.at[0], blocks_in.at[part, from_core], in_recv.at[part, from_core]).wait()

    LINK = {0: z_plus, 1: z_minus, 2: y_plus, 3: y_minus}

    def geometry(part):
        return raw_geometry if part is RAW else slot_geometry

    def unit(part, at_y, at_z, cols):
        return raw.at[at_y, at_z, :, cols] if part is RAW else rows.at[part, at_y, at_z, :, cols]

    def g_send(part, link, event, at_y, at_z, cols):
        piece = unit(part, at_y, at_z, cols)
        pltpu.make_async_remote_copy(
            src_ref=piece, dst_ref=piece,
            send_sem=gather_send.at[part, event], recv_sem=gather_recv.at[part, link, event],
            device_id=LINK[link], device_id_type=MESH,
        ).start()

    def g_wait(part, link, event, cols):
        piece = unit(part, 0, 0, cols)
        pltpu.make_async_copy(piece, piece, gather_recv.at[part, link, event]).wait()

    def gather_own(part):
        @pl.when(part == 0)
        def _():
            wait_in(0, 1 - core)

        @pl.when(part > 0)
        def _():
            wait_in(part, 0)
            wait_in(part, 1)

        first, second = blocks_in[part, 0].astype(F32), blocks_in[part, 1].astype(F32)
        _, ga_cols, gb_cols, _ = slot_geometry
        rows[part, y, z, :, ga_cols] = jnp.concatenate([first[:8], second[:8]], axis=0).astype(BF16)
        rows[part, y, z, :, gb_cols] = jnp.concatenate([first[8:], second[8:]], axis=0).astype(BF16)
        send_own(part)

    def send_own(part):
        for link in range(4):
            g_send(part, link, 0, y, z, geometry(part)[0])

    def gather_a(part):
        whole, ga_cols, gb_cols, g = geometry(part)
        for link in range(4):
            g_wait(part, link, 0, whole)
        g_send(part, 0, 1, y, zm, g[0])
        g_send(part, 1, 1, y, zp, g[1])
        g_send(part, 2, 1, ym, z, g[2])
        g_send(part, 3, 1, yp, z, g[3])
        for link in (2, 3):
            g_send(part, link, 2, y, zm, ga_cols)
        for link in (0, 1):
            g_send(part, link, 2, ym, z, gb_cols)
        for link in (2, 3):
            g_send(part, link, 3, y, zp, ga_cols)
        for link in (0, 1):
            g_send(part, link, 3, yp, z, gb_cols)
        g_send(part, 0, 5, y, zm, g[2])
        g_send(part, 1, 5, y, zp, g[3])
        g_send(part, 2, 5, ym, z, g[0])
        g_send(part, 3, 5, yp, z, g[1])

    def gather_b(part):
        _, ga_cols, gb_cols, g = geometry(part)
        for link in range(4):
            g_wait(part, link, 1, g[link])
        for link in (2, 3):
            g_send(part, link, 4, y, z2, ga_cols)
        for link in (0, 1):
            g_send(part, link, 4, y2, z, gb_cols)

    def gather_on(part, event, of_y, of_z):
        _, ga_cols, _, g = geometry(part)
        for link in range(4):
            g_wait(part, link, event, ga_cols)
        g_send(part, 0, event + 4, of_y, zm, g[2])
        g_send(part, 1, event + 4, of_y, zp, g[3])
        g_send(part, 2, event + 4, ym, of_z, g[0])
        g_send(part, 3, event + 4, yp, of_z, g[1])

    def gather_c(part):
        gather_on(part, 2, ym, zm)
        gather_on(part, 3, yp, zp)

    def gather_d(part):
        gather_on(part, 4, y2, z2)

    def gather_e(part):
        g = geometry(part)[3]
        for event in range(5, 9):
            for link in range(4):
                g_wait(part, link, event, g[(link + 2) % 4])

    def wait_units(sem, part, units):
        piece = rows.at[part, 0, pl.ds(0, units)] if units <= 4 else rows.at[part, pl.ds(0, units // 4)]
        pltpu.make_async_copy(piece, piece, sem).wait()

    def gather_sent(part):
        for event, units in enumerate((4, 1, 2, 2, 2, 1, 1, 1, 1)):
            if part is RAW:
                piece = raw.at[0, pl.ds(0, units)]
            else:
                piece = rows.at[part, 0, pl.ds(0, units), :, slot_geometry[0]]
            pltpu.make_async_copy(piece, piece, gather_send.at[part, event]).wait()

    def fill_slots():
        lane = lax.broadcasted_iota(jnp.int32, (32, 128), 1)

        @pl.loop(0, 16)
        def _(i):
            of_y, of_z = i // 4, i % 4
            where = jnp.concatenate([raw[of_y, of_z, :, pl.ds(2 * extra + 128 * j, 128)] for j in (0, 1)], axis=0)
            where = where.astype(F32).astype(jnp.int32)
            table = jnp.concatenate([(lane == where).astype(F32), (lane == where + 8).astype(F32)], axis=0).astype(BF16)
            lines = [raw[of_y, of_z, :, pl.ds(extra * j + x_half * k, x_half)] for k in (0, 1) for j in (0, 1)]
            filled = lax.dot_general(table, jnp.concatenate(lines, axis=0), FIRST, preferred_element_type=F32)
            slots[:, of_y, of_z] = filled.astype(BF16).reshape(8, 16, x_half)

    def shifted(part, from_core):
        cols = pl.ds(pl.multiple_of(split + from_core * x_half, 128), x_half)
        return rows.at[part, :, :, :, cols]

    def shift_copy(part, to_core):
        dest = ((x + 4 - chip_offset(part)) % 4) * 2 + to_core
        return pltpu.make_async_remote_copy(
            src_ref=slots.at[dest], dst_ref=shifted(part, core),
            send_sem=shift_send.at[part, to_core], recv_sem=shift_recv.at[part, core],
            device_id=(dest, ffn), device_id_type=MESH,
        )

    def shift_home():
        return pltpu.make_async_copy(slots.at[att], shifted(0, core), home_sem)

    def shift(part):
        if part == 0:
            shift_home().start()
            shift_copy(0, 1 - core).start()
        else:
            shift_copy(part, 0).start()
            shift_copy(part, 1).start()

    def wait_shift(part, from_core):
        pltpu.make_async_copy(slots.at[0], shifted(part, from_core), shift_recv.at[part, from_core]).wait()

    def complete(part):
        @pl.when(part == 0)
        def _():
            shift_home().wait()
            wait_shift(0, 1 - core)

        @pl.when(part > 0)
        def _():
            wait_shift(part, 0)
            wait_shift(part, 1)

        @pl.loop(0, 16)
        def _(i):
            of_y, of_z = i // 4, i % 4
            first = rows[part, of_y, of_z, :, split : split + x_half].astype(F32)
            second = rows[part, of_y, of_z, :, split + x_half :].astype(F32)
            rows[part, of_y, of_z, :, split : split + x_half] = (
                jnp.concatenate([first[:8], second[:8]], axis=0).astype(BF16)
            )
            rows[part, of_y, of_z, :, split + x_half :] = (
                jnp.concatenate([first[8:], second[8:]], axis=0).astype(BF16)
            )

    def project(part, lower, upper):
        @pl.loop(lower, upper)
        def _(i):
            cols = pl.ds(pl.multiple_of(i * quarter, quarter), quarter)
            block = rows[part, :, :, :, cols].reshape(256, quarter)
            gate = lax.dot_general(w_gate[:, cols], block, LAST, preferred_element_type=F32)
            up = lax.dot_general(w_up[:, cols], block, LAST, preferred_element_type=F32)

            @pl.when(i == 0)
            def _():
                gate_sum[...] = gate
                up_sum[...] = up

            @pl.when(i > 0)
            def _():
                gate_sum[...] += gate
                up_sum[...] += up

    def activate():
        gate = gate_sum[...]
        mid[...] = (gate / (1.0 + jnp.exp(-gate)) * up_sum[...]).T.astype(BF16)

    def lower_rows(part, lower, upper):
        @pl.loop(lower, upper)
        def _(i):
            cols = pl.ds(pl.multiple_of(i * quarter, quarter), quarter)
            partial = jnp.dot(mid[...], w_down[:, cols], preferred_element_type=F32)
            rows[part, :, :, :, cols] = partial.astype(BF16).reshape(4, 4, 16, quarter)

    def r_send(part, link, event, src, dst):
        pltpu.make_async_remote_copy(
            src_ref=src, dst_ref=dst,
            send_sem=reduce_send.at[part, 3 if event == 9 else event // 4], recv_sem=reduce_recv.at[part, link, event],
            device_id=LINK[link], device_id_type=MESH,
        ).start()

    def r_wait(part, link, event, dst):
        pltpu.make_async_copy(dst, dst, reduce_recv.at[part, link, event]).wait()

    def add(index, *terms):
        total = rows[index].astype(F32)
        for term in terms:
            total = total + term.astype(F32)
        rows[index] = total.astype(BF16)

    across_z, across_y = (z2, zp, zm, z), (y2, yp, ym, y)

    def landing(part):
        return part * 2 // 3

    def reduce_1a(part):
        for i in range(4):
            r_send(part, 2, i, rows.at[part, y2, across_z[i], :, q[0]], near_y1.at[landing(part), 0, i])
            r_send(part, 3, i, rows.at[part, y2, across_z[i], :, q[1]], near_y1.at[landing(part), 1, i])

    def reduce_1b(part):
        for i in range(4):
            r_send(part, 0, i, rows.at[part, across_y[i], z2, :, q[2]], near_z1.at[landing(part), 0, i])
            r_send(part, 1, i, rows.at[part, across_y[i], z2, :, q[3]], near_z1.at[landing(part), 1, i])

    def reduce_2(part):
        for i in range(4):
            at_y, at_z = across_y[i], across_z[i]
            for side, goal in ((0, yp), (1, ym)):
                r_wait(part, 2 + side, i, near_y1.at[landing(part), side, i])
                add((part, goal, at_z, slice(None), q[side]), near_y1[landing(part), side, i])
                r_send(part, 2 + side, 4 + i, rows.at[part, goal, at_z, :, a_cols], near_y2.at[landing(part), side, i])
            for side, goal in ((0, zp), (1, zm)):
                r_wait(part, side, i, near_z1.at[landing(part), side, i])
                add((part, at_y, goal, slice(None), q[2 + side]), near_z1[landing(part), side, i])
                r_send(part, side, 4 + i, rows.at[part, at_y, goal, :, b_cols], near_z2.at[landing(part), side, i])

    def reduce_3(part, pieces):
        for i in pieces:
            at_y, at_z = across_y[i], across_z[i]
            r_wait(part, 2, 4 + i, near_y2.at[landing(part), 0, i])
            r_wait(part, 3, 4 + i, near_y2.at[landing(part), 1, i])
            add((part, y, at_z, slice(None), a_cols), near_y2[landing(part), 0, i], near_y2[landing(part), 1, i])
            r_wait(part, 0, 4 + i, near_z2.at[landing(part), 0, i])
            r_wait(part, 1, 4 + i, near_z2.at[landing(part), 1, i])
            add((part, at_y, z, slice(None), b_cols), near_z2[landing(part), 0, i], near_z2[landing(part), 1, i])
            if i == 0:
                for side in range(2):
                    r_send(part, side, 8, rows.at[part, y, z2, :, q[side]], far_z1.at[landing(part), side])
                    r_send(part, 2 + side, 8, rows.at[part, y2, z, :, q[2 + side]], far_y1.at[landing(part), side])
            elif i < 3:
                side = i - 1
                r_wait(part, side, 8, far_z1.at[landing(part), side])
                add((part, y, at_z, slice(None), q[side]), far_z1[landing(part), side])
                r_send(part, side, 9, rows.at[part, y, at_z, :, a_cols], far_z2.at[landing(part), side])
                r_wait(part, 2 + side, 8, far_y1.at[landing(part), side])
                add((part, at_y, z, slice(None), q[2 + side]), far_y1[landing(part), side])
                r_send(part, 2 + side, 9, rows.at[part, at_y, z, :, b_cols], far_y2.at[landing(part), side])

    def back_copy(part, to_core):
        dest = ((x + chip_offset(part)) % 4) * 2 + to_core
        return pltpu.make_async_remote_copy(
            src_ref=blocks_back.at[part, to_core], dst_ref=returned.at[att],
            send_sem=back_send.at[part, to_core], recv_sem=back_recv.at[att],
            device_id=(dest, ffn), device_id_type=MESH,
        )

    def reduce_5(part):
        for side in range(2):
            r_wait(part, side, 9, far_z2.at[landing(part), side])
            r_wait(part, 2 + side, 9, far_y2.at[landing(part), side])
        left = rows[part, y, z, :, a_cols].astype(F32) + far_z2[landing(part), 0].astype(F32) + far_z2[landing(part), 1].astype(F32)
        right = rows[part, y, z, :, b_cols].astype(F32) + far_y2[landing(part), 0].astype(F32) + far_y2[landing(part), 1].astype(F32)
        for to_core in range(2):
            lines = slice(8 * to_core, 8 * to_core + 8)
            blocks_back[part, to_core] = jnp.concatenate([left[lines], right[lines]], axis=0).astype(BF16)

        if isinstance(part, int) and part == 0:
            back_copy(part, 1 - core).start()
            returned[att] = blocks_back[part, core]
        else:
            back_copy(part, 0).start()
            back_copy(part, 1).start()

        for event, units in enumerate((4, 8, 1, 2)):
            wait_units(reduce_send.at[part, event], part, units)

    send_own(RAW)
    in_copy(0, 1 - core).start()
    for part in range(1, 4):
        for to_core in range(2):
            in_copy(part, to_core).start()
    blocks_in[0, core] = blocks_out[att]
    gather_own(0)
    gather_a(RAW)
    gather_b(RAW)
    gather_c(RAW)
    gather_own(1)
    gather_d(RAW)

    @pl.loop(0, 6)
    def _(step):
        gathering = step < 4
        computing = jnp.logical_and(step >= 1, step < 5)
        sending = jnp.logical_and(step >= 2, step < 5)
        reducing = step >= 3
        at_c, at_r = step - 1, step - 2

        @pl.when(step == 2)
        def _():
            shift(3)

        @pl.when(gathering)
        def _():
            gather_a(step)

        @pl.when(reducing)
        def _():
            reduce_2(at_r % 3)

        @pl.when(step == 4)
        def _():
            reduce_1a(0)
            reduce_1b(0)

        @pl.when(step >= 4)
        def _():
            reduce_5(step - 3)

        @pl.when(computing)
        def _():
            gather_e(at_c)

        @pl.when(step == 0)
        def _():
            gather_e(RAW)
            fill_slots()
            for part in range(3):
                shift(part)

        @pl.when(step == 1)
        def _():
            for load in loads:
                load.wait()

        @pl.when(computing)
        def _():
            complete(at_c)
            project(at_c, 0, 2)

        @pl.when(gathering)
        def _():
            gather_b(step)

        @pl.when(computing)
        def _():
            project(at_c, 2, 4)

        @pl.when(gathering)
        def _():
            gather_c(step)

        @pl.when(step < 2)
        def _():
            gather_own(step + 2)

        @pl.when(computing)
        def _():
            activate()
            gather_sent(at_c)
            lower_rows(at_c, 0, 2)

        @pl.when(sending)
        def _():
            reduce_1a(at_c)

        @pl.when(gathering)
        def _():
            gather_d(step)

        @pl.when(computing)
        def _():
            lower_rows(at_c, 2, 4)

        @pl.when(sending)
        def _():
            reduce_1b(at_c)

        @pl.when(reducing)
        def _():
            reduce_3(at_r, (0,))

        @pl.when(step == 4)
        def _():
            reduce_2(3)

        @pl.when(reducing)
        def _():
            reduce_3(at_r, (1, 2, 3))

        @pl.when(step == 5)
        def _():
            reduce_3(0, (0,))

    reduce_3(0, (1, 2, 3))
    reduce_5(3)
    reduce_5(0)
    gather_sent(RAW)
    shift_copy(0, 1 - core).wait_send()
    in_copy(0, 1 - core).wait_send()
    back_copy(0, 1 - core).wait_send()
    for part in range(1, 4):
        for to_core in range(2):
            shift_copy(part, to_core).wait_send()
            in_copy(part, to_core).wait_send()
            back_copy(part, to_core).wait_send()
    for step in range(1, 8):
        source = (att + step) % 8
        pltpu.make_async_copy(blocks_back.at[0, 0], returned.at[source], back_recv.at[source]).wait()
    lines = returned[...].reshape(128, half)
    out[:, :half] = (
        hidden[:, :half].astype(F32) + lax.dot_general(table_a, lines, FIRST, preferred_element_type=F32)
    ).astype(BF16)
    out[:, half:] = (
        hidden[:, half:].astype(F32) + lax.dot_general(table_b, lines, FIRST, preferred_element_type=F32)
    ).astype(BF16)


def per_device(hidden, route, norm_gain, gate_weight, up_weight, down_weight):
    row_count, width = hidden.shape
    units = gate_weight.shape[2]
    half, quarter = width // 2, width // 4
    extra = raw_columns(width)
    split = width - extra
    vmem, dma = pltpu.VMEM, pltpu.SemaphoreType.DMA
    return pl.pallas_call(
        ffn_kernel,
        out_shape=jax.ShapeDtypeStruct((row_count, width), BF16),
        in_specs=[pl.BlockSpec(memory_space=vmem)] * 3 + [pl.BlockSpec(memory_space=pl.ANY)] * 3,
        out_specs=pl.BlockSpec(memory_space=vmem),
        scratch_shapes=[
            vmem((units, width), BF16),
            vmem((units, width), BF16),
            vmem((units, width), BF16),
            vmem((8, 16, split // 2), BF16),
            vmem((4, 2, 16, split // 2), BF16),
            vmem((4, 2, 16, half), BF16),
            vmem((8, 16, half), BF16),
            vmem((4, 4, 4, 16, width), BF16),
            vmem((4, 4, 16, 2 * extra + 256), BF16),
            vmem((8, 4, 4, 16, extra // 2), BF16),
            vmem((units, 256), F32),
            vmem((units, 256), F32),
            vmem((256, units), BF16),
            vmem((3, 2, 4, 16, quarter), BF16),
            vmem((3, 2, 4, 16, quarter), BF16),
            vmem((3, 2, 4, 16, half), BF16),
            vmem((3, 2, 4, 16, half), BF16),
            vmem((3, 2, 16, quarter), BF16),
            vmem((3, 2, 16, quarter), BF16),
            vmem((3, 2, 16, half), BF16),
            vmem((3, 2, 16, half), BF16),
            dma((3,)),
            dma((4, 2)),
            dma((4, 2)),
            dma((4, 2)),
            dma((4, 2)),
            dma,
            dma((4, 2)),
            dma((8,)),
            dma((5, 9)),
            dma((5, 4, 9)),
            dma((4, 4)),
            dma((4, 4, 10)),
        ],
        compiler_params=pltpu.CompilerParams(
            collective_id=0, has_side_effects=True, vmem_limit_bytes=63 * 1024 * 1024
        ),
    )(
        hidden, route.reshape(1, row_count), norm_gain.reshape(1, width),
        jnp.swapaxes(gate_weight, 1, 2), jnp.swapaxes(up_weight, 1, 2), down_weight,
    )


def solution(mesh):
    placed = (
        P(("att", "ffn"), None),
        P(("att", "ffn"), None),
        P(),
        P("att", None, "ffn"),
        P("att", None, "ffn"),
        P("att", "ffn", None),
    )
    return jax.shard_map(
        per_device, mesh=mesh, in_specs=placed, out_specs=P(("att", "ffn"), None), check_vma=False
    )
```

```python
import functools

import jax
import jax.numpy as jnp
from jax import lax
from jax.experimental import pallas as pl
from jax.experimental.pallas import tpu as pltpu
from jax.sharding import PartitionSpec as P

MESH = pl.DeviceIdType.MESH
F32 = jnp.float32
BF16 = jnp.bfloat16
FIRST = (((0,), (0,)), ((), ()))
LAST = (((1,), (1,)), ((), ()))


RAW = 4

ORDER = (
    4, 88, 8, 12, 1, 92, 2, 16, 96, 20, 5, 9, 24, 13, 17, 3, 28, 21, 6, 32,
    36, 40, 10, 14, 7, 100, 25, 29, 18, 22, 33, 11, 37, 45, 41, 49, 53, 15, 19, 26,
    23, 57, 61, 30, 65, 69, 34, 38, 46, 42, 50, 27, 54, 73, 77, 58, 31, 62, 66, 44,
    35, 70, 39, 47, 81, 48, 43, 51, 85, 55, 59, 63, 74, 67, 71, 78, 52, 56, 60, 64,
    68, 75, 82, 86, 79, 72, 76, 83, 80, 87, 84,
)


def chip_offset(part):
    return part + part // 2 - 2 * (part // 3)


def raw_columns(width):
    return width // 4


def halves(width):
    half = width // 2
    more = (half // 128 + 1) // 2 * 128
    less = half - more
    quarters = [pl.ds(0, more), pl.ds(more, less), pl.ds(half, less), pl.ds(half + less, more)]
    return pl.ds(0, width), pl.ds(0, half), pl.ds(half, half), quarters


def ffn_kernel(
    hidden, route, gain, gate_hbm, up_hbm, down_hbm, out,
    w_gate, w_up, w_down, blocks_out, blocks_back, returned, rows, raw, slots,
    gate_sum, up_sum, mid,
    near_y1, near_z1, near_y2, near_z2, far_z1, far_y1, far_z2, far_y2,
    w_sem, in_send, in_recv, shift_send, shift_recv, home_sem, back_send, back_recv, gather_send, gather_recv, reduce_send, reduce_recv,
):
    att, ffn = lax.axis_index("att"), lax.axis_index("ffn")
    x, core = att // 2, att % 2
    y, z = ffn // 4, ffn % 4
    yp, y2, ym = (y + 1) % 4, (y + 2) % 4, (y + 3) % 4
    zp, z2, zm = (z + 1) % 4, (z + 2) % 4, (z + 3) % 4
    width = hidden.shape[1]
    half, quarter = width // 2, width // 4
    a_cols, b_cols = pl.ds(0, half), pl.ds(half, half)
    q = [pl.ds(i * quarter, quarter) for i in range(4)]
    extra = raw_columns(width)
    split = width - extra
    g_half, x_half = split // 2, extra // 2
    slot_geometry, raw_geometry = halves(split), halves(2 * extra + 256)
    z_plus, z_minus, y_plus, y_minus = (att, y * 4 + zp), (att, y * 4 + zm), (att, yp * 4 + z), (att, ym * 4 + z)
    ALL = pl.ds(0, 4)

    barrier = pltpu.get_barrier_semaphore()
    for other in (z_plus, z_minus, y_plus, y_minus):
        pl.semaphore_signal(barrier, inc=1, device_id=other, device_id_type=MESH)
    for step in range(1, 8):
        pl.semaphore_signal(barrier, inc=1, device_id=((att + step) % 8, ffn), device_id_type=MESH)
    loads = [
        pltpu.make_async_copy(src.at[0], dst, w_sem.at[i])
        for i, (src, dst) in enumerate(((gate_hbm, w_gate), (up_hbm, w_up), (down_hbm, w_down)))
    ]
    for load in loads:
        load.start()

    widened = hidden[...].astype(F32)
    scale = lax.rsqrt(jnp.mean(widened * widened, axis=-1, keepdims=True) + 1e-06)
    normed = (widened * scale * gain[...]).astype(BF16)
    member = (lax.broadcasted_iota(jnp.int32, (8, 32), 0) == route[...]).astype(F32)
    earlier = (
        lax.broadcasted_iota(jnp.int32, (32, 32), 0) < lax.broadcasted_iota(jnp.int32, (32, 32), 1)
    ).astype(F32)
    before = jnp.dot(member, earlier, preferred_element_type=F32)
    rank = jnp.sum(before * member, axis=0, keepdims=True).astype(jnp.int32)
    place = route[...] * 16 + rank
    line = lax.broadcasted_iota(jnp.int32, (128, 32), 0)
    table_a = (line == place).astype(F32).astype(BF16)
    table_b = (line == place + 8).astype(F32).astype(BF16)
    placed = jnp.dot(table_a, normed[:, :g_half], preferred_element_type=F32)
    placed = placed + jnp.dot(table_b, normed[:, g_half:split], preferred_element_type=F32)
    blocks_out[...] = placed.astype(BF16).reshape(8, 16, g_half)
    number = jnp.broadcast_to(place.astype(F32), (128, 32)).T.astype(BF16)
    for i in range(2):
        lines = slice(16 * i, 16 * i + 16)
        raw[y, z, :, extra * i : extra * (i + 1)] = normed[lines, split:]
        raw[y, z, :, 2 * extra + 128 * i : 2 * extra + 128 * (i + 1)] = number[lines]

    pl.semaphore_wait(barrier, 11)

    def arrival(part, from_core):
        return rows.at[part, y, z, :, pl.ds(pl.multiple_of(from_core * g_half, 128), g_half)]

    def in_copy(part, to_core):
        dest = ((x + 4 - chip_offset(part)) % 4) * 2 + to_core
        return pltpu.make_async_remote_copy(
            src_ref=blocks_out.at[dest], dst_ref=arrival(part, core),
            send_sem=in_send.at[part, to_core], recv_sem=in_recv.at[part, core],
            device_id=(dest, ffn), device_id_type=MESH,
        )

    def wait_in(part, from_core):
        pltpu.make_async_copy(blocks_out.at[0], arrival(part, from_core), in_recv.at[part, from_core]).wait()

    LINK = {0: z_plus, 1: z_minus, 2: y_plus, 3: y_minus}

    def geometry(part):
        return raw_geometry if part is RAW else slot_geometry

    def unit(part, at_y, at_z, cols):
        return raw.at[at_y, at_z, :, cols] if part is RAW else rows.at[part, at_y, at_z, :, cols]

    def g_send(part, link, event, at_y, at_z, cols):
        piece = unit(part, at_y, at_z, cols)
        pltpu.make_async_remote_copy(
            src_ref=piece, dst_ref=piece,
            send_sem=gather_send.at[part, event], recv_sem=gather_recv.at[part, link, event],
            device_id=LINK[link], device_id_type=MESH,
        ).start()

    def g_wait(part, link, event, cols):
        piece = unit(part, 0, 0, cols)
        pltpu.make_async_copy(piece, piece, gather_recv.at[part, link, event]).wait()

    def gather_own(part):
        @pl.when(part == 0)
        def _():
            wait_in(0, 1 - core)

        @pl.when(part > 0)
        def _():
            wait_in(part, 0)
            wait_in(part, 1)

        _, ga_cols, gb_cols, _ = slot_geometry
        first, second = rows[part, y, z, :, ga_cols].astype(F32), rows[part, y, z, :, gb_cols].astype(F32)
        rows[part, y, z, :, ga_cols] = jnp.concatenate([first[:8], second[:8]], axis=0).astype(BF16)
        rows[part, y, z, :, gb_cols] = jnp.concatenate([first[8:], second[8:]], axis=0).astype(BF16)
        send_own(part)

    def send_own(part):
        for link in range(4):
            g_send(part, link, 0, y, z, geometry(part)[0])

    def gather_a(part):
        whole, ga_cols, gb_cols, g = geometry(part)
        for link in range(4):
            g_wait(part, link, 0, whole)
        g_send(part, 0, 1, y, zm, g[0])
        g_send(part, 1, 1, y, zp, g[1])
        g_send(part, 2, 1, ym, z, g[2])
        g_send(part, 3, 1, yp, z, g[3])
        for link in (2, 3):
            g_send(part, link, 2, y, zm, ga_cols)
        for link in (0, 1):
            g_send(part, link, 2, ym, z, gb_cols)
        for link in (2, 3):
            g_send(part, link, 3, y, zp, ga_cols)
        for link in (0, 1):
            g_send(part, link, 3, yp, z, gb_cols)
        g_send(part, 0, 5, y, zm, g[2])
        g_send(part, 1, 5, y, zp, g[3])
        g_send(part, 2, 5, ym, z, g[0])
        g_send(part, 3, 5, yp, z, g[1])

    def gather_b(part):
        _, ga_cols, gb_cols, g = geometry(part)
        for link in range(4):
            g_wait(part, link, 1, g[link])
        for link in (2, 3):
            g_send(part, link, 4, y, z2, ga_cols)
        for link in (0, 1):
            g_send(part, link, 4, y2, z, gb_cols)

    def gather_on(part, event, of_y, of_z):
        _, ga_cols, _, g = geometry(part)
        for link in range(4):
            g_wait(part, link, event, ga_cols)
        g_send(part, 0, event + 4, of_y, zm, g[2])
        g_send(part, 1, event + 4, of_y, zp, g[3])
        g_send(part, 2, event + 4, ym, of_z, g[0])
        g_send(part, 3, event + 4, yp, of_z, g[1])

    def gather_c(part):
        gather_on(part, 2, ym, zm)

    def gather_d(part):
        gather_on(part, 3, yp, zp)

    def gather_f(part):
        gather_on(part, 4, y2, z2)

    def gather_e(part):
        g = geometry(part)[3]
        for event in range(5, 9):
            for link in range(4):
                g_wait(part, link, event, g[(link + 2) % 4])

    def wait_units(sem, part, units):
        piece = rows.at[part, 0, pl.ds(0, units)] if units <= 4 else rows.at[part, pl.ds(0, units // 4)]
        pltpu.make_async_copy(piece, piece, sem).wait()

    def gather_sent(part):
        for event, units in enumerate((4, 1, 2, 2, 2, 1, 1, 1, 1)):
            if part is RAW:
                piece = raw.at[0, pl.ds(0, units)]
            else:
                piece = rows.at[part, 0, pl.ds(0, units), :, slot_geometry[0]]
            pltpu.make_async_copy(piece, piece, gather_send.at[part, event]).wait()

    def fill_slots():
        lane = lax.broadcasted_iota(jnp.int32, (32, 128), 1)

        @pl.loop(0, 16)
        def _(i):
            of_y, of_z = i // 4, i % 4
            where = jnp.concatenate([raw[of_y, of_z, :, pl.ds(2 * extra + 128 * j, 128)] for j in (0, 1)], axis=0)
            where = where.astype(F32).astype(jnp.int32)
            table = jnp.concatenate([(lane == where).astype(F32), (lane == where + 8).astype(F32)], axis=0).astype(BF16)
            lines = [raw[of_y, of_z, :, pl.ds(extra * j + x_half * k, x_half)] for k in (0, 1) for j in (0, 1)]
            filled = lax.dot_general(table, jnp.concatenate(lines, axis=0), FIRST, preferred_element_type=F32)
            slots[:, of_y, of_z] = filled.astype(BF16).reshape(8, 16, x_half)

    def shifted(part, from_core):
        cols = pl.ds(pl.multiple_of(split + from_core * x_half, 128), x_half)
        return rows.at[part, :, :, :, cols]

    def shift_copy(part, to_core):
        dest = ((x + 4 - chip_offset(part)) % 4) * 2 + to_core
        return pltpu.make_async_remote_copy(
            src_ref=slots.at[dest], dst_ref=shifted(part, core),
            send_sem=shift_send.at[part, to_core], recv_sem=shift_recv.at[part, core],
            device_id=(dest, ffn), device_id_type=MESH,
        )

    def shift_home():
        return pltpu.make_async_copy(slots.at[att], shifted(0, core), home_sem)

    def shift(part):
        if part == 0:
            shift_home().start()
            shift_copy(0, 1 - core).start()
        else:
            shift_copy(part, 0).start()
            shift_copy(part, 1).start()

    def wait_shift(part, from_core):
        pltpu.make_async_copy(slots.at[0], shifted(part, from_core), shift_recv.at[part, from_core]).wait()

    def complete(part):
        @pl.when(part == 0)
        def _():
            shift_home().wait()
            wait_shift(0, 1 - core)

        @pl.when(part > 0)
        def _():
            wait_shift(part, 0)
            wait_shift(part, 1)

        @pl.loop(0, 16)
        def _(i):
            of_y, of_z = i // 4, i % 4
            first = rows[part, of_y, of_z, :, split : split + x_half].astype(F32)
            second = rows[part, of_y, of_z, :, split + x_half :].astype(F32)
            rows[part, of_y, of_z, :, split : split + x_half] = (
                jnp.concatenate([first[:8], second[:8]], axis=0).astype(BF16)
            )
            rows[part, of_y, of_z, :, split + x_half :] = (
                jnp.concatenate([first[8:], second[8:]], axis=0).astype(BF16)
            )

    def project(part, lower):
        @pl.loop(lower, lower + 2)
        def _(i):
            cols = pl.ds(pl.multiple_of(i * quarter, quarter), quarter)
            block = rows[part, :, :, :, cols].reshape(256, quarter)
            gate = lax.dot_general(w_gate[:, cols], block, LAST, preferred_element_type=F32)
            up = lax.dot_general(w_up[:, cols], block, LAST, preferred_element_type=F32)

            @pl.when(i == 0)
            def _():
                gate_sum[...] = gate
                up_sum[...] = up

            @pl.when(i > 0)
            def _():
                gate_sum[...] += gate
                up_sum[...] += up

    def activate():
        gate = gate_sum[...]
        mid[...] = (gate / (1.0 + jnp.exp(-gate)) * up_sum[...]).T.astype(BF16)

    def lower_rows(part, lower):
        @pl.loop(lower, lower + 2)
        def _(i):
            cols = pl.ds(pl.multiple_of(i * quarter, quarter), quarter)
            partial = jnp.dot(mid[...], w_down[:, cols], preferred_element_type=F32)
            rows[part, :, :, :, cols] = partial.astype(BF16).reshape(4, 4, 16, quarter)

    def r_send(part, link, event, src, dst):
        pltpu.make_async_remote_copy(
            src_ref=src, dst_ref=dst,
            send_sem=reduce_send.at[part, 3 if event == 9 else event // 4], recv_sem=reduce_recv.at[part, link, event],
            device_id=LINK[link], device_id_type=MESH,
        ).start()

    def r_wait(part, link, event, dst):
        pltpu.make_async_copy(dst, dst, reduce_recv.at[part, link, event]).wait()

    def add(index, *terms):
        total = rows[index].astype(F32)
        for term in terms:
            total = total + term.astype(F32)
        rows[index] = total.astype(BF16)

    across_z, across_y = (z2, zp, zm, z), (y2, yp, ym, y)

    def landing(part):
        return part * 2 // 3

    def reduce_1a(part):
        for i in range(4):
            r_send(part, 2, i, rows.at[part, y2, across_z[i], :, q[0]], near_y1.at[landing(part), 0, i])
            r_send(part, 3, i, rows.at[part, y2, across_z[i], :, q[1]], near_y1.at[landing(part), 1, i])

    def reduce_1b(part):
        for i in range(4):
            r_send(part, 0, i, rows.at[part, across_y[i], z2, :, q[2]], near_z1.at[landing(part), 0, i])
            r_send(part, 1, i, rows.at[part, across_y[i], z2, :, q[3]], near_z1.at[landing(part), 1, i])

    def reduce_2(part, pieces):
        for i in pieces:
            at_y, at_z = across_y[i], across_z[i]
            for side, goal in ((0, yp), (1, ym)):
                r_wait(part, 2 + side, i, near_y1.at[landing(part), side, i])
                add((part, goal, at_z, slice(None), q[side]), near_y1[landing(part), side, i])
                r_send(part, 2 + side, 4 + i, rows.at[part, goal, at_z, :, a_cols], near_y2.at[landing(part), side, i])
            for side, goal in ((0, zp), (1, zm)):
                r_wait(part, side, i, near_z1.at[landing(part), side, i])
                add((part, at_y, goal, slice(None), q[2 + side]), near_z1[landing(part), side, i])
                r_send(part, side, 4 + i, rows.at[part, at_y, goal, :, b_cols], near_z2.at[landing(part), side, i])

    def reduce_3(part, pieces):
        for i in pieces:
            at_y, at_z = across_y[i], across_z[i]
            r_wait(part, 2, 4 + i, near_y2.at[landing(part), 0, i])
            r_wait(part, 3, 4 + i, near_y2.at[landing(part), 1, i])
            add((part, y, at_z, slice(None), a_cols), near_y2[landing(part), 0, i], near_y2[landing(part), 1, i])
            r_wait(part, 0, 4 + i, near_z2.at[landing(part), 0, i])
            r_wait(part, 1, 4 + i, near_z2.at[landing(part), 1, i])
            add((part, at_y, z, slice(None), b_cols), near_z2[landing(part), 0, i], near_z2[landing(part), 1, i])
            if i == 0:
                for side in range(2):
                    r_send(part, side, 8, rows.at[part, y, z2, :, q[side]], far_z1.at[landing(part), side])
                    r_send(part, 2 + side, 8, rows.at[part, y2, z, :, q[2 + side]], far_y1.at[landing(part), side])
            elif i < 3:
                side = i - 1
                r_wait(part, side, 8, far_z1.at[landing(part), side])
                add((part, y, at_z, slice(None), q[side]), far_z1[landing(part), side])
                r_send(part, side, 9, rows.at[part, y, at_z, :, a_cols], far_z2.at[landing(part), side])
                r_wait(part, 2 + side, 8, far_y1.at[landing(part), side])
                add((part, at_y, z, slice(None), q[2 + side]), far_y1[landing(part), side])
                r_send(part, 2 + side, 9, rows.at[part, at_y, z, :, b_cols], far_y2.at[landing(part), side])

    def back_copy(part, to_core):
        dest = ((x + chip_offset(part)) % 4) * 2 + to_core
        return pltpu.make_async_remote_copy(
            src_ref=blocks_back.at[part, to_core], dst_ref=returned.at[att],
            send_sem=back_send.at[part, to_core], recv_sem=back_recv.at[att],
            device_id=(dest, ffn), device_id_type=MESH,
        )

    def reduce_5(part):
        for side in range(2):
            r_wait(part, side, 9, far_z2.at[landing(part), side])
            r_wait(part, 2 + side, 9, far_y2.at[landing(part), side])
        left = rows[part, y, z, :, a_cols].astype(F32) + far_z2[landing(part), 0].astype(F32) + far_z2[landing(part), 1].astype(F32)
        right = rows[part, y, z, :, b_cols].astype(F32) + far_y2[landing(part), 0].astype(F32) + far_y2[landing(part), 1].astype(F32)
        for to_core in range(2):
            lines = slice(8 * to_core, 8 * to_core + 8)
            blocks_back[part, to_core] = jnp.concatenate([left[lines], right[lines]], axis=0).astype(BF16)

        @pl.when(part == 0)
        def _():
            back_copy(part, 1 - core).start()
            returned[att] = blocks_back[part, core]

        @pl.when(part > 0)
        def _():
            back_copy(part, 0).start()
            back_copy(part, 1).start()

        for event, units in enumerate((4, 8, 1, 2)):
            wait_units(reduce_send.at[part, event], part, units)

    send_own(RAW)
    in_copy(0, 1 - core).start()
    for part in range(1, 4):
        for to_core in range(2):
            in_copy(part, to_core).start()
    rows[0, y, z, :, pl.ds(pl.multiple_of(core * g_half, 128), g_half)] = blocks_out[att]
    gather_own(0)
    gather_a(RAW)
    gather_b(RAW)
    gather_c(RAW)
    gather_d(RAW)

    def products(part, second):
        @pl.when(jnp.logical_not(second))
        def _():
            complete(part)

        project(part, jnp.where(second, 2, 0))

    def lowering(part, second):
        @pl.when(jnp.logical_not(second))
        def _():
            activate()
            gather_sent(part)

        lower_rows(part, jnp.where(second, 2, 0))

    def spread(part):
        for load in loads:
            load.wait()
        fill_slots()
        for part in range(3):
            shift(part)

    steps = [
        gather_own, gather_a, gather_b, gather_c, gather_d, gather_f, gather_e,
        products, products, lowering, lowering, reduce_1a, reduce_1b,
        *[functools.partial(reduce_2, pieces=(i,)) for i in range(4)],
        *[functools.partial(reduce_3, pieces=(i,)) for i in range(4)],
        reduce_5,
        lambda part: gather_f(RAW), lambda part: gather_e(RAW), spread, lambda part: shift(3),
    ]

    def take(kind, part, low, high):
        if high - low == 1:
            steps[low](part)
        elif steps[low] is steps[high - 1]:
            steps[low](part, kind > low)
        else:
            middle = (low + high) // 2
            if steps[middle] is steps[middle - 1]:
                middle += 1
            lax.cond(
                kind < middle, lambda: take(kind, part, low, middle), lambda: take(kind, part, middle, high)
            )

    per_word = 4
    words = [sum(code << (7 * k) for k, code in enumerate(ORDER[i : i + per_word])) for i in range(0, len(ORDER), per_word)]

    @pl.loop(0, len(ORDER))
    def _(step):
        at = step // per_word
        word = jnp.int32(words[0])
        for i in range(1, len(words)):
            word = jnp.where(at == i, jnp.int32(words[i]), word)
        code = lax.shift_right_logical(word, 7 * (step % per_word)) % 128
        take(code // 4, code % 4, 0, len(steps))

    gather_sent(RAW)
    shift_copy(0, 1 - core).wait_send()
    in_copy(0, 1 - core).wait_send()
    back_copy(0, 1 - core).wait_send()
    for part in range(1, 4):
        for to_core in range(2):
            shift_copy(part, to_core).wait_send()
            in_copy(part, to_core).wait_send()
            back_copy(part, to_core).wait_send()
    for step in range(1, 8):
        source = (att + step) % 8
        pltpu.make_async_copy(blocks_back.at[0, 0], returned.at[source], back_recv.at[source]).wait()
    lines = returned[...].reshape(128, half)
    out[:, :half] = (
        hidden[:, :half].astype(F32) + lax.dot_general(table_a, lines, FIRST, preferred_element_type=F32)
    ).astype(BF16)
    out[:, half:] = (
        hidden[:, half:].astype(F32) + lax.dot_general(table_b, lines, FIRST, preferred_element_type=F32)
    ).astype(BF16)


def per_device(hidden, route, norm_gain, gate_weight, up_weight, down_weight):
    row_count, width = hidden.shape
    units = gate_weight.shape[2]
    half, quarter = width // 2, width // 4
    extra = raw_columns(width)
    split = width - extra
    vmem, dma = pltpu.VMEM, pltpu.SemaphoreType.DMA
    return pl.pallas_call(
        ffn_kernel,
        out_shape=jax.ShapeDtypeStruct((row_count, width), BF16),
        in_specs=[pl.BlockSpec(memory_space=vmem)] * 3 + [pl.BlockSpec(memory_space=pl.ANY)] * 3,
        out_specs=pl.BlockSpec(memory_space=vmem),
        scratch_shapes=[
            vmem((units, width), BF16),
            vmem((units, width), BF16),
            vmem((units, width), BF16),
            vmem((8, 16, split // 2), BF16),
            vmem((4, 2, 16, half), BF16),
            vmem((8, 16, half), BF16),
            vmem((4, 4, 4, 16, width), BF16),
            vmem((4, 4, 16, 2 * extra + 256), BF16),
            vmem((8, 4, 4, 16, extra // 2), BF16),
            vmem((units, 256), F32),
            vmem((units, 256), F32),
            vmem((256, units), BF16),
            vmem((3, 2, 4, 16, quarter), BF16),
            vmem((3, 2, 4, 16, quarter), BF16),
            vmem((3, 2, 4, 16, half), BF16),
            vmem((3, 2, 4, 16, half), BF16),
            vmem((3, 2, 16, quarter), BF16),
            vmem((3, 2, 16, quarter), BF16),
            vmem((3, 2, 16, half), BF16),
            vmem((3, 2, 16, half), BF16),
            dma((3,)),
            dma((4, 2)),
            dma((4, 2)),
            dma((4, 2)),
            dma((4, 2)),
            dma,
            dma((4, 2)),
            dma((8,)),
            dma((5, 9)),
            dma((5, 4, 9)),
            dma((4, 4)),
            dma((4, 4, 10)),
        ],
        compiler_params=pltpu.CompilerParams(
            collective_id=0, has_side_effects=True, vmem_limit_bytes=63 * 1024 * 1024
        ),
    )(
        hidden, route.reshape(1, row_count), norm_gain.reshape(1, width),
        jnp.swapaxes(gate_weight, 1, 2), jnp.swapaxes(up_weight, 1, 2), down_weight,
    )


def solution(mesh):
    placed = (
        P(("att", "ffn"), None),
        P(("att", "ffn"), None),
        P(),
        P("att", None, "ffn"),
        P("att", None, "ffn"),
        P("att", "ffn", None),
    )
    return jax.shard_map(
        per_device, mesh=mesh, in_specs=placed, out_specs=P(("att", "ffn"), None), check_vma=False
    )
```

```python
import functools

import jax
import jax.numpy as jnp
from jax import lax
from jax.experimental import pallas as pl
from jax.experimental.pallas import tpu as pltpu
from jax.sharding import PartitionSpec as P

MESH = pl.DeviceIdType.MESH
F32 = jnp.float32
BF16 = jnp.bfloat16
FIRST = (((0,), (0,)), ((), ()))
LAST = (((1,), (1,)), ((), ()))


RAW = 4

ORDER = (
    4, 88, 8, 1, 92, 12, 16, 96, 20, 5, 9, 2, 24, 28, 13, 17, 32, 21, 6, 36,
    10, 25, 100, 3, 40, 14, 29, 18, 33, 22, 7, 37, 41, 45, 49, 11, 26, 30, 53, 57,
    34, 15, 38, 19, 61, 23, 65, 42, 46, 50, 69, 27, 31, 54, 58, 62, 66, 44, 35, 48,
    39, 43, 70, 73, 77, 47, 51, 74, 78, 81, 85, 55, 59, 63, 67, 82, 71, 86, 52, 56,
    75, 79, 60, 64, 83, 104, 108, 112, 68, 116, 120, 124, 128, 87, 132, 72, 76, 80, 136, 140,
    144, 84, 148,
)


def chip_offset(part):
    return part + part // 2 - 2 * (part // 3)


def raw_columns(width):
    return width // 4


def halves(width):
    half = width // 2
    more = (half // 128 + 1) // 2 * 128
    less = half - more
    quarters = [pl.ds(0, more), pl.ds(more, less), pl.ds(half, less), pl.ds(half + less, more)]
    return pl.ds(0, width), pl.ds(0, half), pl.ds(half, half), quarters


def ffn_kernel(
    hidden, route, gain, gate_hbm, up_hbm, down_hbm, out,
    w_gate, w_up, w_down, blocks_out, blocks_back, returned, rows, raw, slots,
    gate_sum, up_sum, mid,
    near_y1, near_z1, near_y2, near_z2, far_z1, far_y1, far_z2, far_y2,
    w_sem, in_send, in_recv, shift_send, shift_recv, home_sem, column_send, column_recv, free_sem, back_send, back_recv, gather_send, gather_recv, reduce_send, reduce_recv,
):
    att, ffn = lax.axis_index("att"), lax.axis_index("ffn")
    x, core = att // 2, att % 2
    y, z = ffn // 4, ffn % 4
    yp, y2, ym = (y + 1) % 4, (y + 2) % 4, (y + 3) % 4
    zp, z2, zm = (z + 1) % 4, (z + 2) % 4, (z + 3) % 4
    width = hidden.shape[1]
    quarter = width // 4
    extra = raw_columns(width)
    split = width - extra
    g_half, x_half = split // 2, extra // 2
    slot_geometry, raw_geometry, sum_geometry = halves(split), halves(2 * extra + 256), halves(2 * extra)
    z_plus, z_minus, y_plus, y_minus = (att, y * 4 + zp), (att, y * 4 + zm), (att, yp * 4 + z), (att, ym * 4 + z)
    ALL = pl.ds(0, 4)

    barrier = pltpu.get_barrier_semaphore()
    for other in (z_plus, z_minus, y_plus, y_minus):
        pl.semaphore_signal(barrier, inc=1, device_id=other, device_id_type=MESH)
    for step in range(1, 8):
        pl.semaphore_signal(barrier, inc=1, device_id=((att + step) % 8, ffn), device_id_type=MESH)
    loads = [
        pltpu.make_async_copy(src.at[0], dst, w_sem.at[i])
        for i, (src, dst) in enumerate(((gate_hbm, w_gate), (up_hbm, w_up), (down_hbm, w_down)))
    ]
    for load in loads:
        load.start()

    widened = hidden[...].astype(F32)
    scale = lax.rsqrt(jnp.mean(widened * widened, axis=-1, keepdims=True) + 1e-06)
    normed = (widened * scale * gain[...]).astype(BF16)
    member = (lax.broadcasted_iota(jnp.int32, (8, 32), 0) == route[...]).astype(F32)
    earlier = (
        lax.broadcasted_iota(jnp.int32, (32, 32), 0) < lax.broadcasted_iota(jnp.int32, (32, 32), 1)
    ).astype(F32)
    before = jnp.dot(member, earlier, preferred_element_type=F32)
    rank = jnp.sum(before * member, axis=0, keepdims=True).astype(jnp.int32)
    place = route[...] * 16 + rank
    line = lax.broadcasted_iota(jnp.int32, (128, 32), 0)
    table_a = (line == place).astype(F32).astype(BF16)
    table_b = (line == place + 8).astype(F32).astype(BF16)
    placed = jnp.dot(table_a, normed[:, :g_half], preferred_element_type=F32)
    placed = placed + jnp.dot(table_b, normed[:, g_half:split], preferred_element_type=F32)
    blocks_out[...] = placed.astype(BF16).reshape(8, 16, g_half)
    number = jnp.broadcast_to(place.astype(F32), (128, 32)).T.astype(BF16)
    for i in range(2):
        lines = slice(16 * i, 16 * i + 16)
        raw[y, z, :, extra * i : extra * (i + 1)] = normed[lines, split:]
        raw[y, z, :, 2 * extra + 128 * i : 2 * extra + 128 * (i + 1)] = number[lines]

    pl.semaphore_wait(barrier, 11)

    def arrival(part, from_core):
        return rows.at[part, y, z, :, pl.ds(pl.multiple_of(from_core * g_half, 128), g_half)]

    def in_copy(part, to_core):
        dest = ((x + 4 - chip_offset(part)) % 4) * 2 + to_core
        return pltpu.make_async_remote_copy(
            src_ref=blocks_out.at[dest], dst_ref=arrival(part, core),
            send_sem=in_send.at[part, to_core], recv_sem=in_recv.at[part, core],
            device_id=(dest, ffn), device_id_type=MESH,
        )

    def wait_in(part, from_core):
        pltpu.make_async_copy(blocks_out.at[0], arrival(part, from_core), in_recv.at[part, from_core]).wait()

    LINK = {0: z_plus, 1: z_minus, 2: y_plus, 3: y_minus}

    def geometry(part):
        return raw_geometry if part is RAW else slot_geometry

    def unit(part, at_y, at_z, cols):
        return raw.at[at_y, at_z, :, cols] if part is RAW else rows.at[part, at_y, at_z, :, cols]

    def g_send(part, link, event, at_y, at_z, cols):
        piece = unit(part, at_y, at_z, cols)
        pltpu.make_async_remote_copy(
            src_ref=piece, dst_ref=piece,
            send_sem=gather_send.at[part, event], recv_sem=gather_recv.at[part, link, event],
            device_id=LINK[link], device_id_type=MESH,
        ).start()

    def g_wait(part, link, event, cols):
        piece = unit(part, 0, 0, cols)
        pltpu.make_async_copy(piece, piece, gather_recv.at[part, link, event]).wait()

    def gather_own(part):
        @pl.when(part == 0)
        def _():
            wait_in(0, 1 - core)

        @pl.when(part > 0)
        def _():
            wait_in(part, 0)
            wait_in(part, 1)

        _, ga_cols, gb_cols, _ = slot_geometry
        first, second = rows[part, y, z, :, ga_cols].astype(F32), rows[part, y, z, :, gb_cols].astype(F32)
        rows[part, y, z, :, ga_cols] = jnp.concatenate([first[:8], second[:8]], axis=0).astype(BF16)
        rows[part, y, z, :, gb_cols] = jnp.concatenate([first[8:], second[8:]], axis=0).astype(BF16)
        send_own(part)

    def send_own(part):
        for link in range(4):
            g_send(part, link, 0, y, z, geometry(part)[0])

    def gather_a(part):
        whole, ga_cols, gb_cols, g = geometry(part)
        for link in range(4):
            g_wait(part, link, 0, whole)
        g_send(part, 0, 1, y, zm, g[0])
        g_send(part, 1, 1, y, zp, g[1])
        g_send(part, 2, 1, ym, z, g[2])
        g_send(part, 3, 1, yp, z, g[3])
        for link in (2, 3):
            g_send(part, link, 2, y, zm, ga_cols)
        for link in (0, 1):
            g_send(part, link, 2, ym, z, gb_cols)
        for link in (2, 3):
            g_send(part, link, 3, y, zp, ga_cols)
        for link in (0, 1):
            g_send(part, link, 3, yp, z, gb_cols)
        g_send(part, 0, 5, y, zm, g[2])
        g_send(part, 1, 5, y, zp, g[3])
        g_send(part, 2, 5, ym, z, g[0])
        g_send(part, 3, 5, yp, z, g[1])

    def gather_b(part):
        _, ga_cols, gb_cols, g = geometry(part)
        for link in range(4):
            g_wait(part, link, 1, g[link])
        for link in (2, 3):
            g_send(part, link, 4, y, z2, ga_cols)
        for link in (0, 1):
            g_send(part, link, 4, y2, z, gb_cols)

    def gather_on(part, event, of_y, of_z):
        _, ga_cols, _, g = geometry(part)
        for link in range(4):
            g_wait(part, link, event, ga_cols)
        g_send(part, 0, event + 4, of_y, zm, g[2])
        g_send(part, 1, event + 4, of_y, zp, g[3])
        g_send(part, 2, event + 4, ym, of_z, g[0])
        g_send(part, 3, event + 4, yp, of_z, g[1])

    def gather_c(part):
        gather_on(part, 2, ym, zm)

    def gather_d(part):
        gather_on(part, 3, yp, zp)

    def gather_f(part):
        gather_on(part, 4, y2, z2)

    def gather_e(part):
        g = geometry(part)[3]
        for event in range(5, 9):
            for link in range(4):
                g_wait(part, link, event, g[(link + 2) % 4])

    def gather_sent(part):
        for event, units in enumerate((4, 1, 2, 2, 2, 1, 1, 1, 1)):
            if part is RAW:
                piece = raw.at[0, pl.ds(0, units)]
            else:
                piece = rows.at[part, 0, pl.ds(0, units), :, slot_geometry[0]]
            pltpu.make_async_copy(piece, piece, gather_send.at[part, event]).wait()

    def slot_table(of_y, of_z, lane):
        where = jnp.concatenate([raw[of_y, of_z, :, pl.ds(2 * extra + 128 * j, 128)] for j in (0, 1)], axis=0)
        where = where.astype(F32).astype(jnp.int32)
        return jnp.concatenate([(lane == where).astype(F32), (lane == where + 8).astype(F32)], axis=0).astype(BF16)

    def fill_slots():
        lane = lax.broadcasted_iota(jnp.int32, (32, 128), 1)

        @pl.loop(0, 16)
        def _(i):
            of_y, of_z = i // 4, i % 4
            table = slot_table(of_y, of_z, lane)
            lines = [raw[of_y, of_z, :, pl.ds(extra * j + x_half * k, x_half)] for k in (0, 1) for j in (0, 1)]
            filled = lax.dot_general(table, jnp.concatenate(lines, axis=0), FIRST, preferred_element_type=F32)
            slots[:, of_y, of_z] = filled.astype(BF16).reshape(8, 16, x_half)

    def shifted(part, from_core):
        cols = pl.ds(pl.multiple_of(split + from_core * x_half, 128), x_half)
        return rows.at[part, :, :, :, cols]

    def shift_copy(part, to_core):
        dest = ((x + 4 - chip_offset(part)) % 4) * 2 + to_core
        return pltpu.make_async_remote_copy(
            src_ref=slots.at[dest], dst_ref=shifted(part, core),
            send_sem=shift_send.at[part, to_core], recv_sem=shift_recv.at[part, core],
            device_id=(dest, ffn), device_id_type=MESH,
        )

    def shift_home():
        return pltpu.make_async_copy(slots.at[att], shifted(0, core), home_sem)

    def shift(part):
        if part == 0:
            shift_home().start()
            shift_copy(0, 1 - core).start()
        else:
            shift_copy(part, 0).start()
            shift_copy(part, 1).start()

    def wait_shift(part, from_core):
        pltpu.make_async_copy(slots.at[0], shifted(part, from_core), shift_recv.at[part, from_core]).wait()

    def complete(part):
        @pl.when(part == 0)
        def _():
            shift_home().wait()
            wait_shift(0, 1 - core)

        @pl.when(part > 0)
        def _():
            wait_shift(part, 0)
            wait_shift(part, 1)

        complete_again(part)

    def complete_again(part):
        @pl.loop(0, 16)
        def _(i):
            of_y, of_z = i // 4, i % 4
            first = rows[part, of_y, of_z, :, split : split + x_half].astype(F32)
            second = rows[part, of_y, of_z, :, split + x_half :].astype(F32)
            rows[part, of_y, of_z, :, split : split + x_half] = (
                jnp.concatenate([first[:8], second[:8]], axis=0).astype(BF16)
            )
            rows[part, of_y, of_z, :, split + x_half :] = (
                jnp.concatenate([first[8:], second[8:]], axis=0).astype(BF16)
            )

    def project(part, lower):
        @pl.loop(lower, lower + 2)
        def _(i):
            cols = pl.ds(pl.multiple_of(i * quarter, quarter), quarter)
            block = rows[part, :, :, :, cols].reshape(256, quarter)
            gate = lax.dot_general(w_gate[:, cols], block, LAST, preferred_element_type=F32)
            up = lax.dot_general(w_up[:, cols], block, LAST, preferred_element_type=F32)

            @pl.when(i == 0)
            def _():
                gate_sum[...] = gate
                up_sum[...] = up

            @pl.when(i > 0)
            def _():
                gate_sum[...] += gate
                up_sum[...] += up

    def activate():
        gate = gate_sum[...]
        mid[...] = (gate / (1.0 + jnp.exp(-gate)) * up_sum[...]).T.astype(BF16)

    def lower_rows(part, lower):
        @pl.loop(lower, lower + 2)
        def _(step):
            cols = pl.ds(pl.multiple_of((3 - step) * quarter, quarter), quarter)
            partial = jnp.dot(mid[...], w_down[:, cols], preferred_element_type=F32)
            rows[part, :, :, :, cols] = partial.astype(BF16).reshape(4, 4, 16, quarter)

    def sums(part):
        return sum_geometry if part is RAW else slot_geometry

    def landing(part):
        return 1 if part is RAW else part * 2 // 3

    def place_at(buffer, part, cols, *index):
        return buffer.at[(landing(part), *index, slice(None), pl.ds(0, cols.size))]

    def r_send(part, link, event, src, dst):
        pltpu.make_async_remote_copy(
            src_ref=src, dst_ref=dst,
            send_sem=reduce_send.at[part, 3 if event == 9 else event // 4], recv_sem=reduce_recv.at[part, link, event],
            device_id=LINK[link], device_id_type=MESH,
        ).start()

    def r_wait(part, link, event, dst):
        pltpu.make_async_copy(dst, dst, reduce_recv.at[part, link, event]).wait()

    def add(piece, *terms):
        total = piece[...].astype(F32)
        for term in terms:
            total = total + term[...].astype(F32)
        piece[...] = total.astype(BF16)

    across_z, across_y = (z2, zp, zm, z), (y2, yp, ym, y)

    def reduce_1a(part):
        q = sums(part)[3]
        for i in range(4):
            for side in range(2):
                cols = q[side]
                r_send(part, 2 + side, i, unit(part, y2, across_z[i], cols), place_at(near_y1, part, cols, side, i))

    def reduce_1b(part):
        q = sums(part)[3]
        for i in range(4):
            for side in range(2):
                cols = q[2 + side]
                r_send(part, side, i, unit(part, across_y[i], z2, cols), place_at(near_z1, part, cols, side, i))

    def reduce_2(part, pieces):
        _, a_cols, b_cols, q = sums(part)
        for i in pieces:
            at_y, at_z = across_y[i], across_z[i]
            for side, goal in ((0, yp), (1, ym)):
                landed = place_at(near_y1, part, q[side], side, i)
                r_wait(part, 2 + side, i, landed)
                add(unit(part, goal, at_z, q[side]), landed)
                r_send(part, 2 + side, 4 + i, unit(part, goal, at_z, a_cols), place_at(near_y2, part, a_cols, side, i))
            for side, goal in ((0, zp), (1, zm)):
                landed = place_at(near_z1, part, q[2 + side], side, i)
                r_wait(part, side, i, landed)
                add(unit(part, at_y, goal, q[2 + side]), landed)
                r_send(part, side, 4 + i, unit(part, at_y, goal, b_cols), place_at(near_z2, part, b_cols, side, i))

    def reduce_3(part, pieces):
        _, a_cols, b_cols, q = sums(part)
        for i in pieces:
            at_y, at_z = across_y[i], across_z[i]
            landed = [place_at(near_y2, part, a_cols, side, i) for side in range(2)]
            r_wait(part, 2, 4 + i, landed[0])
            r_wait(part, 3, 4 + i, landed[1])
            add(unit(part, y, at_z, a_cols), *landed)
            landed = [place_at(near_z2, part, b_cols, side, i) for side in range(2)]
            r_wait(part, 0, 4 + i, landed[0])
            r_wait(part, 1, 4 + i, landed[1])
            add(unit(part, at_y, z, b_cols), *landed)
            if i == 0:
                for side in range(2):
                    r_send(part, side, 8, unit(part, y, z2, q[side]), place_at(far_z1, part, q[side], side))
                    cols = q[2 + side]
                    r_send(part, 2 + side, 8, unit(part, y2, z, cols), place_at(far_y1, part, cols, side))
            elif i < 3:
                side = i - 1
                landed = place_at(far_z1, part, q[side], side)
                r_wait(part, side, 8, landed)
                add(unit(part, y, at_z, q[side]), landed)
                r_send(part, side, 9, unit(part, y, at_z, a_cols), place_at(far_z2, part, a_cols, side))
                landed = place_at(far_y1, part, q[2 + side], side)
                r_wait(part, 2 + side, 8, landed)
                add(unit(part, at_y, z, q[2 + side]), landed)
                r_send(part, 2 + side, 9, unit(part, at_y, z, b_cols), place_at(far_y2, part, b_cols, side))

    def back_copy(part, to_core):
        dest = ((x + chip_offset(part)) % 4) * 2 + to_core
        return pltpu.make_async_remote_copy(
            src_ref=blocks_back.at[part, to_core], dst_ref=returned.at[att],
            send_sem=back_send.at[part, to_core], recv_sem=back_recv.at[att],
            device_id=(dest, ffn), device_id_type=MESH,
        )

    def reduce_5(part):
        whole, a_cols, b_cols, _ = sums(part)
        left, right = unit(part, y, z, a_cols)[...].astype(F32), unit(part, y, z, b_cols)[...].astype(F32)
        for side in range(2):
            landed = place_at(far_z2, part, a_cols, side)
            r_wait(part, side, 9, landed)
            left = left + landed[...].astype(F32)
            landed = place_at(far_y2, part, b_cols, side)
            r_wait(part, 2 + side, 9, landed)
            right = right + landed[...].astype(F32)
        if part is RAW:
            out[:16, split:] = (hidden[:16, split:].astype(F32) + left.astype(BF16).astype(F32)).astype(BF16)
            out[16:, split:] = (hidden[16:, split:].astype(F32) + right.astype(BF16).astype(F32)).astype(BF16)
        else:
            for to_core in range(2):
                lines = slice(8 * to_core, 8 * to_core + 8)
                blocks_back[part, to_core] = jnp.concatenate([left[lines], right[lines]], axis=0).astype(BF16)

            @pl.when(part == 0)
            def _():
                back_copy(part, 1 - core).start()
                returned[att] = blocks_back[part, core]

            @pl.when(part > 0)
            def _():
                back_copy(part, 0).start()
                back_copy(part, 1).start()

        for event, units in enumerate((4, 8, 1, 2)):
            many = (0, pl.ds(0, units)) if units <= 4 else (pl.ds(0, units // 4),)
            if part is RAW:
                piece = raw_units(many, whole)
            else:
                piece = part_units(part, many, whole)
            pltpu.make_async_copy(piece, piece, reduce_send.at[part, event]).wait()

    def raw_units(many, cols):
        return raw.at[many[0], many[1], :, cols] if len(many) == 2 else raw.at[many[0], :, :, cols]

    def part_units(part, many, cols):
        return rows.at[part, many[0], many[1], :, cols] if len(many) == 2 else rows.at[part, many[0], :, :, cols]

    def column_copy(part, to_core):
        dest = ((x + chip_offset(part)) % 4) * 2 + to_core
        return pltpu.make_async_remote_copy(
            src_ref=shifted(part, to_core), dst_ref=slots.at[att],
            send_sem=column_send.at[part, to_core], recv_sem=column_recv.at[att],
            device_id=(dest, ffn), device_id_type=MESH,
        )

    def column_home():
        return pltpu.make_async_copy(shifted(0, core), slots.at[att], home_sem)

    def free_slots(part):
        def free(to_core):
            dest = ((x + 4 - chip_offset(part)) % 4) * 2 + to_core
            shift_copy(part, to_core).wait_send()
            pl.semaphore_signal(free_sem.at[att], inc=1, device_id=(dest, ffn), device_id_type=MESH)

        @pl.when(part == 0)
        def _():
            free(1 - core)

        @pl.when(part > 0)
        def _():
            free(0)
            free(1)

    def return_columns(part):
        complete_again(part)

        @pl.when(part == 0)
        def _():
            column_home().start()
            pl.semaphore_wait(free_sem.at[x * 2 + 1 - core], 1)
            column_copy(0, 1 - core).start()

        @pl.when(part > 0)
        def _():
            for to_core in range(2):
                pl.semaphore_wait(free_sem.at[((x + chip_offset(part)) % 4) * 2 + to_core], 1)
                column_copy(part, to_core).start()

    def collect():
        column_home().wait()
        for step in range(1, 8):
            source = (att + step) % 8
            pltpu.make_async_copy(slots.at[0], slots.at[source], column_recv.at[source]).wait()
        gather_sent(RAW)
        lane = lax.broadcasted_iota(jnp.int32, (32, 128), 1)

        @pl.loop(0, 16)
        def _(i):
            of_y, of_z = i // 4, i % 4
            table = slot_table(of_y, of_z, lane)
            lines = slots[:, of_y, of_z].reshape(128, x_half)
            sums_of = jnp.dot(table, lines, preferred_element_type=F32).astype(BF16)
            for j in range(2):
                for k in range(2):
                    start = 32 * k + 16 * j
                    raw[of_y, of_z, :, pl.ds(extra * j + x_half * k, x_half)] = sums_of[start : start + 16]

    send_own(RAW)
    in_copy(0, 1 - core).start()
    for part in range(1, 4):
        for to_core in range(2):
            in_copy(part, to_core).start()
    rows[0, y, z, :, pl.ds(pl.multiple_of(core * g_half, 128), g_half)] = blocks_out[att]
    gather_own(0)
    gather_a(RAW)
    gather_b(RAW)
    gather_c(RAW)
    gather_d(RAW)

    def products(part, second):
        @pl.when(jnp.logical_not(second))
        def _():
            complete(part)
            free_slots(part)

        project(part, jnp.where(second, 2, 0))

    def lowering(part, second):
        @pl.when(jnp.logical_not(second))
        def _():
            activate()
            gather_sent(part)

        lower_rows(part, jnp.where(second, 2, 0))

        @pl.when(jnp.logical_not(second))
        def _():
            return_columns(part)

    def spread(part):
        for load in loads:
            load.wait()
        fill_slots()
        for part in range(3):
            shift(part)

    steps = [
        gather_own, gather_a, gather_b, gather_c, gather_d, gather_f, gather_e,
        products, products, lowering, lowering, reduce_1a, reduce_1b,
        *[functools.partial(reduce_2, pieces=(i,)) for i in range(4)],
        *[functools.partial(reduce_3, pieces=(i,)) for i in range(4)],
        reduce_5,
        lambda part: gather_f(RAW), lambda part: gather_e(RAW), spread, lambda part: shift(3),
        lambda part: collect(), lambda part: reduce_1a(RAW), lambda part: reduce_1b(RAW),
        *[lambda part, i=i: reduce_2(RAW, (i,)) for i in range(4)],
        *[lambda part, i=i: reduce_3(RAW, (i,)) for i in range(4)],
        lambda part: reduce_5(RAW),
    ]

    def take(kind, part, low, high):
        if high - low == 1:
            steps[low](part)
        elif steps[low] is steps[high - 1]:
            steps[low](part, kind > low)
        else:
            middle = (low + high) // 2
            if steps[middle] is steps[middle - 1]:
                middle += 1
            lax.cond(
                kind < middle, lambda: take(kind, part, low, middle), lambda: take(kind, part, middle, high)
            )

    per_word = 3
    words = [sum(code << (8 * k) for k, code in enumerate(ORDER[i : i + per_word])) for i in range(0, len(ORDER), per_word)]

    @pl.loop(0, len(ORDER))
    def _(step):
        at = step // per_word
        word = jnp.int32(words[0])
        for i in range(1, len(words)):
            word = jnp.where(at == i, jnp.int32(words[i]), word)
        code = lax.shift_right_logical(word, 8 * (step % per_word)) % 256
        take(code // 4, code % 4, 0, len(steps))

    column_copy(0, 1 - core).wait_send()
    in_copy(0, 1 - core).wait_send()
    back_copy(0, 1 - core).wait_send()
    for part in range(1, 4):
        for to_core in range(2):
            column_copy(part, to_core).wait_send()
            in_copy(part, to_core).wait_send()
            back_copy(part, to_core).wait_send()
    for step in range(1, 8):
        source = (att + step) % 8
        pltpu.make_async_copy(blocks_back.at[0, 0], returned.at[source], back_recv.at[source]).wait()
    lines = returned[...].reshape(128, g_half)
    for table, cols in ((table_a, slice(0, g_half)), (table_b, slice(g_half, split))):
        found = lax.dot_general(table, lines, FIRST, preferred_element_type=F32)
        out[:, cols] = (hidden[:, cols].astype(F32) + found).astype(BF16)


def per_device(hidden, route, norm_gain, gate_weight, up_weight, down_weight):
    row_count, width = hidden.shape
    units = gate_weight.shape[2]
    extra = raw_columns(width)
    split = width - extra
    more = halves(split)[3][0].size
    vmem, dma = pltpu.VMEM, pltpu.SemaphoreType.DMA
    return pl.pallas_call(
        ffn_kernel,
        out_shape=jax.ShapeDtypeStruct((row_count, width), BF16),
        in_specs=[pl.BlockSpec(memory_space=vmem)] * 3 + [pl.BlockSpec(memory_space=pl.ANY)] * 3,
        out_specs=pl.BlockSpec(memory_space=vmem),
        scratch_shapes=[
            vmem((units, width), BF16),
            vmem((units, width), BF16),
            vmem((units, width), BF16),
            vmem((8, 16, split // 2), BF16),
            vmem((4, 2, 16, split // 2), BF16),
            vmem((8, 16, split // 2), BF16),
            vmem((4, 4, 4, 16, width), BF16),
            vmem((4, 4, 16, 2 * extra + 256), BF16),
            vmem((8, 4, 4, 16, extra // 2), BF16),
            vmem((units, 256), F32),
            vmem((units, 256), F32),
            vmem((256, units), BF16),
            vmem((3, 2, 4, 16, more), BF16),
            vmem((3, 2, 4, 16, more), BF16),
            vmem((3, 2, 4, 16, split // 2), BF16),
            vmem((3, 2, 4, 16, split // 2), BF16),
            vmem((3, 2, 16, more), BF16),
            vmem((3, 2, 16, more), BF16),
            vmem((3, 2, 16, split // 2), BF16),
            vmem((3, 2, 16, split // 2), BF16),
            dma((3,)),
            dma((4, 2)),
            dma((4, 2)),
            dma((4, 2)),
            dma((4, 2)),
            dma,
            dma((4, 2)),
            dma((8,)),
            pltpu.SemaphoreType.REGULAR((8,)),
            dma((4, 2)),
            dma((8,)),
            dma((5, 9)),
            dma((5, 4, 9)),
            dma((5, 4)),
            dma((5, 4, 10)),
        ],
        compiler_params=pltpu.CompilerParams(
            collective_id=0, has_side_effects=True, vmem_limit_bytes=63 * 1024 * 1024
        ),
    )(
        hidden, route.reshape(1, row_count), norm_gain.reshape(1, width),
        jnp.swapaxes(gate_weight, 1, 2), jnp.swapaxes(up_weight, 1, 2), down_weight,
    )


def solution(mesh):
    placed = (
        P(("att", "ffn"), None),
        P(("att", "ffn"), None),
        P(),
        P("att", None, "ffn"),
        P("att", None, "ffn"),
        P("att", "ffn", None),
    )
    return jax.shard_map(
        per_device, mesh=mesh, in_specs=placed, out_specs=P(("att", "ffn"), None), check_vma=False
    )
```

```python
import functools

import jax
import jax.numpy as jnp
from jax import lax
from jax.experimental import pallas as pl
from jax.experimental.pallas import tpu as pltpu
from jax.sharding import PartitionSpec as P

MESH = pl.DeviceIdType.MESH
F32 = jnp.float32
BF16 = jnp.bfloat16
FIRST = (((0,), (0,)), ((), ()))
LAST = (((1,), (1,)), ((), ()))


RAW = 4

ORDER = (
    4, 88, 8, 1, 92, 12, 16, 96, 20, 5, 9, 2, 24, 28, 13, 17, 32, 21, 6, 36,
    10, 25, 100, 3, 40, 14, 29, 18, 33, 22, 7, 37, 41, 45, 49, 11, 26, 30, 53, 57,
    34, 15, 38, 19, 61, 23, 65, 42, 46, 50, 69, 27, 31, 54, 58, 62, 66, 44, 35, 48,
    39, 43, 70, 73, 77, 47, 51, 74, 78, 81, 85, 55, 59, 63, 67, 82, 71, 86, 52, 56,
    75, 79, 60, 64, 83, 104, 108, 112, 68, 116, 120, 124, 128, 87, 132, 72, 76, 80, 136, 140,
    144, 84,
)


def chip_offset(part):
    return part + part // 2 - 2 * (part // 3)


def raw_columns(width):
    return width // 4


def halves(width):
    half = width // 2
    more = (half // 128 + 1) // 2 * 128
    less = half - more
    quarters = [pl.ds(0, more), pl.ds(more, less), pl.ds(half, less), pl.ds(half + less, more)]
    return pl.ds(0, width), pl.ds(0, half), pl.ds(half, half), quarters


def ffn_kernel(
    hidden_hbm, route, gain, gate_hbm, up_hbm, down_hbm, out,
    w_gate, w_up, w_down, blocks_out, blocks_back, returned, rows, raw, slots, hidden,
    gate_sum, up_sum, mid,
    near_y1, near_z1, near_y2, near_z2, far_z1, far_y1, far_z2, far_y2,
    w_sem, in_send, in_recv, shift_send, shift_recv, home_sem, column_send, column_recv, free_sem, back_send, back_recv, gather_send, gather_recv, reduce_send, reduce_recv,
):
    att, ffn = lax.axis_index("att"), lax.axis_index("ffn")
    x, core = att // 2, att % 2
    y, z = ffn // 4, ffn % 4
    yp, y2, ym = (y + 1) % 4, (y + 2) % 4, (y + 3) % 4
    zp, z2, zm = (z + 1) % 4, (z + 2) % 4, (z + 3) % 4
    width = hidden_hbm.shape[1]
    quarter = width // 4
    extra = raw_columns(width)
    split = width - extra
    g_half, x_half = split // 2, extra // 2
    slot_geometry, raw_geometry, sum_geometry = halves(split), halves(2 * extra + 256), halves(2 * extra)
    z_plus, z_minus, y_plus, y_minus = (att, y * 4 + zp), (att, y * 4 + zm), (att, yp * 4 + z), (att, ym * 4 + z)
    ALL = pl.ds(0, 4)

    fetch = pltpu.make_async_copy(hidden_hbm, hidden, home_sem)
    fetch.start()
    barrier = pltpu.get_barrier_semaphore()
    for other in (z_plus, z_minus, y_plus, y_minus):
        pl.semaphore_signal(barrier, inc=1, device_id=other, device_id_type=MESH)
    for step in range(1, 8):
        pl.semaphore_signal(barrier, inc=1, device_id=((att + step) % 8, ffn), device_id_type=MESH)
    loads = [
        pltpu.make_async_copy(src.at[0], dst, w_sem.at[i])
        for i, (src, dst) in enumerate(((gate_hbm, w_gate), (up_hbm, w_up), (down_hbm, w_down)))
    ]
    for load in loads:
        load.start()

    fetch.wait()
    widened = hidden[...].astype(F32)
    scale = lax.rsqrt(jnp.mean(widened * widened, axis=-1, keepdims=True) + 1e-06)
    normed = (widened * scale * gain[...]).astype(BF16)
    member = (lax.broadcasted_iota(jnp.int32, (8, 32), 0) == route[...]).astype(F32)
    earlier = (
        lax.broadcasted_iota(jnp.int32, (32, 32), 0) < lax.broadcasted_iota(jnp.int32, (32, 32), 1)
    ).astype(F32)
    before = jnp.dot(member, earlier, preferred_element_type=F32)
    rank = jnp.sum(before * member, axis=0, keepdims=True).astype(jnp.int32)
    place = route[...] * 16 + rank
    line = lax.broadcasted_iota(jnp.int32, (128, 32), 0)
    table_a = (line == place).astype(F32).astype(BF16)
    table_b = (line == place + 8).astype(F32).astype(BF16)
    placed = jnp.dot(table_a, normed[:, :g_half], preferred_element_type=F32)
    placed = placed + jnp.dot(table_b, normed[:, g_half:split], preferred_element_type=F32)
    blocks_out[...] = placed.astype(BF16).reshape(8, 16, g_half)
    number = jnp.broadcast_to(place.astype(F32), (128, 32)).T.astype(BF16)
    for i in range(2):
        lines = slice(16 * i, 16 * i + 16)
        raw[y, z, :, extra * i : extra * (i + 1)] = normed[lines, split:]
        raw[y, z, :, 2 * extra + 128 * i : 2 * extra + 128 * (i + 1)] = number[lines]

    pl.semaphore_wait(barrier, 11)

    def arrival(part, from_core):
        return rows.at[part, y, z, :, pl.ds(pl.multiple_of(from_core * g_half, 128), g_half)]

    def in_copy(part, to_core):
        dest = ((x + 4 - chip_offset(part)) % 4) * 2 + to_core
        return pltpu.make_async_remote_copy(
            src_ref=blocks_out.at[dest], dst_ref=arrival(part, core),
            send_sem=in_send.at[part, to_core], recv_sem=in_recv.at[part, core],
            device_id=(dest, ffn), device_id_type=MESH,
        )

    def wait_in(part, from_core):
        pltpu.make_async_copy(blocks_out.at[0], arrival(part, from_core), in_recv.at[part, from_core]).wait()

    LINK = {0: z_plus, 1: z_minus, 2: y_plus, 3: y_minus}

    def geometry(part):
        return raw_geometry if part is RAW else slot_geometry

    def unit(part, at_y, at_z, cols):
        return raw.at[at_y, at_z, :, cols] if part is RAW else rows.at[part, at_y, at_z, :, cols]

    def g_send(part, link, event, at_y, at_z, cols):
        piece = unit(part, at_y, at_z, cols)
        pltpu.make_async_remote_copy(
            src_ref=piece, dst_ref=piece,
            send_sem=gather_send.at[part, event], recv_sem=gather_recv.at[part, link, event],
            device_id=LINK[link], device_id_type=MESH,
        ).start()

    def g_wait(part, link, event, cols):
        piece = unit(part, 0, 0, cols)
        pltpu.make_async_copy(piece, piece, gather_recv.at[part, link, event]).wait()

    def gather_own(part):
        @pl.when(part == 0)
        def _():
            wait_in(0, 1 - core)

        @pl.when(part > 0)
        def _():
            wait_in(part, 0)
            wait_in(part, 1)

        _, ga_cols, gb_cols, _ = slot_geometry
        first, second = rows[part, y, z, :, ga_cols].astype(F32), rows[part, y, z, :, gb_cols].astype(F32)
        rows[part, y, z, :, ga_cols] = jnp.concatenate([first[:8], second[:8]], axis=0).astype(BF16)
        rows[part, y, z, :, gb_cols] = jnp.concatenate([first[8:], second[8:]], axis=0).astype(BF16)
        send_own(part)

    def send_own(part):
        for link in range(4):
            g_send(part, link, 0, y, z, geometry(part)[0])

    def gather_a(part):
        whole, ga_cols, gb_cols, g = geometry(part)
        for link in range(4):
            g_wait(part, link, 0, whole)
        g_send(part, 0, 1, y, zm, g[0])
        g_send(part, 1, 1, y, zp, g[1])
        g_send(part, 2, 1, ym, z, g[2])
        g_send(part, 3, 1, yp, z, g[3])
        for link in (2, 3):
            g_send(part, link, 2, y, zm, ga_cols)
        for link in (0, 1):
            g_send(part, link, 2, ym, z, gb_cols)
        for link in (2, 3):
            g_send(part, link, 3, y, zp, ga_cols)
        for link in (0, 1):
            g_send(part, link, 3, yp, z, gb_cols)
        g_send(part, 0, 5, y, zm, g[2])
        g_send(part, 1, 5, y, zp, g[3])
        g_send(part, 2, 5, ym, z, g[0])
        g_send(part, 3, 5, yp, z, g[1])

    def gather_b(part):
        _, ga_cols, gb_cols, g = geometry(part)
        for link in range(4):
            g_wait(part, link, 1, g[link])
        for link in (2, 3):
            g_send(part, link, 4, y, z2, ga_cols)
        for link in (0, 1):
            g_send(part, link, 4, y2, z, gb_cols)

    def gather_on(part, event, of_y, of_z):
        _, ga_cols, _, g = geometry(part)
        for link in range(4):
            g_wait(part, link, event, ga_cols)
        g_send(part, 0, event + 4, of_y, zm, g[2])
        g_send(part, 1, event + 4, of_y, zp, g[3])
        g_send(part, 2, event + 4, ym, of_z, g[0])
        g_send(part, 3, event + 4, yp, of_z, g[1])

    def gather_c(part):
        gather_on(part, 2, ym, zm)

    def gather_d(part):
        gather_on(part, 3, yp, zp)

    def gather_f(part):
        gather_on(part, 4, y2, z2)

    def gather_e(part):
        g = geometry(part)[3]
        for event in range(5, 9):
            for link in range(4):
                g_wait(part, link, event, g[(link + 2) % 4])

    def gather_sent(part):
        for event, units in enumerate((4, 1, 2, 2, 2, 1, 1, 1, 1)):
            if part is RAW:
                piece = raw.at[0, pl.ds(0, units)]
            else:
                piece = rows.at[part, 0, pl.ds(0, units), :, slot_geometry[0]]
            pltpu.make_async_copy(piece, piece, gather_send.at[part, event]).wait()

    def slot_table(of_y, of_z, lane):
        where = jnp.concatenate([raw[of_y, of_z, :, pl.ds(2 * extra + 128 * j, 128)] for j in (0, 1)], axis=0)
        where = where.astype(F32).astype(jnp.int32)
        return jnp.concatenate([(lane == where).astype(F32), (lane == where + 8).astype(F32)], axis=0).astype(BF16)

    def fill_slots():
        lane = lax.broadcasted_iota(jnp.int32, (32, 128), 1)

        @pl.loop(0, 16)
        def _(i):
            of_y, of_z = i // 4, i % 4
            table = slot_table(of_y, of_z, lane)
            lines = [raw[of_y, of_z, :, pl.ds(extra * j + x_half * k, x_half)] for k in (0, 1) for j in (0, 1)]
            filled = lax.dot_general(table, jnp.concatenate(lines, axis=0), FIRST, preferred_element_type=F32)
            slots[:, of_y, of_z] = filled.astype(BF16).reshape(8, 16, x_half)

    def shifted(part, from_core):
        cols = pl.ds(pl.multiple_of(split + from_core * x_half, 128), x_half)
        return rows.at[part, :, :, :, cols]

    def shift_copy(part, to_core):
        dest = ((x + 4 - chip_offset(part)) % 4) * 2 + to_core
        return pltpu.make_async_remote_copy(
            src_ref=slots.at[dest], dst_ref=shifted(part, core),
            send_sem=shift_send.at[part, to_core], recv_sem=shift_recv.at[part, core],
            device_id=(dest, ffn), device_id_type=MESH,
        )

    def shift_home():
        return pltpu.make_async_copy(slots.at[att], shifted(0, core), home_sem)

    def shift(part):
        if part == 0:
            shift_home().start()
            shift_copy(0, 1 - core).start()
        else:
            shift_copy(part, 0).start()
            shift_copy(part, 1).start()

    def wait_shift(part, from_core):
        pltpu.make_async_copy(slots.at[0], shifted(part, from_core), shift_recv.at[part, from_core]).wait()

    def complete(part):
        @pl.when(part == 0)
        def _():
            shift_home().wait()
            wait_shift(0, 1 - core)

        @pl.when(part > 0)
        def _():
            wait_shift(part, 0)
            wait_shift(part, 1)

        complete_again(part)

    def complete_again(part):
        @pl.loop(0, 16)
        def _(i):
            of_y, of_z = i // 4, i % 4
            first = rows[part, of_y, of_z, :, split : split + x_half].astype(F32)
            second = rows[part, of_y, of_z, :, split + x_half :].astype(F32)
            rows[part, of_y, of_z, :, split : split + x_half] = (
                jnp.concatenate([first[:8], second[:8]], axis=0).astype(BF16)
            )
            rows[part, of_y, of_z, :, split + x_half :] = (
                jnp.concatenate([first[8:], second[8:]], axis=0).astype(BF16)
            )

    def project(part, lower):
        @pl.loop(lower, lower + 2)
        def _(i):
            cols = pl.ds(pl.multiple_of(i * quarter, quarter), quarter)
            block = rows[part, :, :, :, cols].reshape(256, quarter)
            gate = lax.dot_general(w_gate[:, cols], block, LAST, preferred_element_type=F32)
            up = lax.dot_general(w_up[:, cols], block, LAST, preferred_element_type=F32)

            @pl.when(i == 0)
            def _():
                gate_sum[...] = gate
                up_sum[...] = up

            @pl.when(i > 0)
            def _():
                gate_sum[...] += gate
                up_sum[...] += up

    def activate():
        gate = gate_sum[...]
        mid[...] = (gate / (1.0 + jnp.exp(-gate)) * up_sum[...]).T.astype(BF16)

    def lower_rows(part, lower):
        @pl.loop(lower, lower + 2)
        def _(step):
            cols = pl.ds(pl.multiple_of((3 - step) * quarter, quarter), quarter)
            partial = jnp.dot(mid[...], w_down[:, cols], preferred_element_type=F32)
            rows[part, :, :, :, cols] = partial.astype(BF16).reshape(4, 4, 16, quarter)

    def sums(part):
        return sum_geometry if part is RAW else slot_geometry

    def landing(part):
        return 1 if part is RAW else part * 2 // 3

    def place_at(buffer, part, cols, *index):
        return buffer.at[(landing(part), *index, slice(None), pl.ds(0, cols.size))]

    def r_send(part, link, event, src, dst):
        pltpu.make_async_remote_copy(
            src_ref=src, dst_ref=dst,
            send_sem=reduce_send.at[part, 3 if event == 9 else event // 4], recv_sem=reduce_recv.at[part, link, event],
            device_id=LINK[link], device_id_type=MESH,
        ).start()

    def r_wait(part, link, event, dst):
        pltpu.make_async_copy(dst, dst, reduce_recv.at[part, link, event]).wait()

    def add(piece, *terms):
        total = piece[...].astype(F32)
        for term in terms:
            total = total + term[...].astype(F32)
        piece[...] = total.astype(BF16)

    across_z, across_y = (z2, zp, zm, z), (y2, yp, ym, y)

    def reduce_1a(part):
        q = sums(part)[3]
        for i in range(4):
            for side in range(2):
                cols = q[side]
                r_send(part, 2 + side, i, unit(part, y2, across_z[i], cols), place_at(near_y1, part, cols, side, i))

    def reduce_1b(part):
        q = sums(part)[3]
        for i in range(4):
            for side in range(2):
                cols = q[2 + side]
                r_send(part, side, i, unit(part, across_y[i], z2, cols), place_at(near_z1, part, cols, side, i))

    def reduce_2(part, pieces):
        _, a_cols, b_cols, q = sums(part)
        for i in pieces:
            at_y, at_z = across_y[i], across_z[i]
            for side, goal in ((0, yp), (1, ym)):
                landed = place_at(near_y1, part, q[side], side, i)
                r_wait(part, 2 + side, i, landed)
                add(unit(part, goal, at_z, q[side]), landed)
                r_send(part, 2 + side, 4 + i, unit(part, goal, at_z, a_cols), place_at(near_y2, part, a_cols, side, i))
            for side, goal in ((0, zp), (1, zm)):
                landed = place_at(near_z1, part, q[2 + side], side, i)
                r_wait(part, side, i, landed)
                add(unit(part, at_y, goal, q[2 + side]), landed)
                r_send(part, side, 4 + i, unit(part, at_y, goal, b_cols), place_at(near_z2, part, b_cols, side, i))

    def reduce_3(part, pieces):
        _, a_cols, b_cols, q = sums(part)
        for i in pieces:
            at_y, at_z = across_y[i], across_z[i]
            landed = [place_at(near_y2, part, a_cols, side, i) for side in range(2)]
            r_wait(part, 2, 4 + i, landed[0])
            r_wait(part, 3, 4 + i, landed[1])
            add(unit(part, y, at_z, a_cols), *landed)
            landed = [place_at(near_z2, part, b_cols, side, i) for side in range(2)]
            r_wait(part, 0, 4 + i, landed[0])
            r_wait(part, 1, 4 + i, landed[1])
            add(unit(part, at_y, z, b_cols), *landed)
            if i == 0:
                for side in range(2):
                    r_send(part, side, 8, unit(part, y, z2, q[side]), place_at(far_z1, part, q[side], side))
                    cols = q[2 + side]
                    r_send(part, 2 + side, 8, unit(part, y2, z, cols), place_at(far_y1, part, cols, side))
            elif i < 3:
                side = i - 1
                landed = place_at(far_z1, part, q[side], side)
                r_wait(part, side, 8, landed)
                add(unit(part, y, at_z, q[side]), landed)
                r_send(part, side, 9, unit(part, y, at_z, a_cols), place_at(far_z2, part, a_cols, side))
                landed = place_at(far_y1, part, q[2 + side], side)
                r_wait(part, 2 + side, 8, landed)
                add(unit(part, at_y, z, q[2 + side]), landed)
                r_send(part, 2 + side, 9, unit(part, at_y, z, b_cols), place_at(far_y2, part, b_cols, side))

    def back_copy(part, to_core):
        dest = ((x + chip_offset(part)) % 4) * 2 + to_core
        return pltpu.make_async_remote_copy(
            src_ref=blocks_back.at[part, to_core], dst_ref=returned.at[att],
            send_sem=back_send.at[part, to_core], recv_sem=back_recv.at[att],
            device_id=(dest, ffn), device_id_type=MESH,
        )

    def reduce_5(part):
        whole, a_cols, b_cols, _ = sums(part)
        left, right = unit(part, y, z, a_cols)[...].astype(F32), unit(part, y, z, b_cols)[...].astype(F32)
        for side in range(2):
            landed = place_at(far_z2, part, a_cols, side)
            r_wait(part, side, 9, landed)
            left = left + landed[...].astype(F32)
            landed = place_at(far_y2, part, b_cols, side)
            r_wait(part, 2 + side, 9, landed)
            right = right + landed[...].astype(F32)
        if part is RAW:
            out[:16, split:] = (hidden[:16, split:].astype(F32) + left.astype(BF16).astype(F32)).astype(BF16)
            out[16:, split:] = (hidden[16:, split:].astype(F32) + right.astype(BF16).astype(F32)).astype(BF16)
        else:
            for to_core in range(2):
                lines = slice(8 * to_core, 8 * to_core + 8)
                blocks_back[part, to_core] = jnp.concatenate([left[lines], right[lines]], axis=0).astype(BF16)

            @pl.when(part == 0)
            def _():
                back_copy(part, 1 - core).start()
                returned[att] = blocks_back[part, core]

            @pl.when(part > 0)
            def _():
                back_copy(part, 0).start()
                back_copy(part, 1).start()

        for event, units in enumerate((4, 8, 1, 2)):
            many = (0, pl.ds(0, units)) if units <= 4 else (pl.ds(0, units // 4),)
            if part is RAW:
                piece = raw_units(many, whole)
            else:
                piece = part_units(part, many, whole)
            pltpu.make_async_copy(piece, piece, reduce_send.at[part, event]).wait()

    def raw_units(many, cols):
        return raw.at[many[0], many[1], :, cols] if len(many) == 2 else raw.at[many[0], :, :, cols]

    def part_units(part, many, cols):
        return rows.at[part, many[0], many[1], :, cols] if len(many) == 2 else rows.at[part, many[0], :, :, cols]

    def column_copy(part, to_core):
        dest = ((x + chip_offset(part)) % 4) * 2 + to_core
        return pltpu.make_async_remote_copy(
            src_ref=shifted(part, to_core), dst_ref=slots.at[att],
            send_sem=column_send.at[part, to_core], recv_sem=column_recv.at[att],
            device_id=(dest, ffn), device_id_type=MESH,
        )

    def column_home():
        return pltpu.make_async_copy(shifted(0, core), slots.at[att], home_sem)

    def free_slots(part):
        def free(to_core):
            dest = ((x + 4 - chip_offset(part)) % 4) * 2 + to_core
            shift_copy(part, to_core).wait_send()
            pl.semaphore_signal(free_sem.at[att], inc=1, device_id=(dest, ffn), device_id_type=MESH)

        @pl.when(part == 0)
        def _():
            free(1 - core)

        @pl.when(part > 0)
        def _():
            free(0)
            free(1)

    def return_columns(part):
        complete_again(part)

        @pl.when(part == 0)
        def _():
            column_home().start()
            pl.semaphore_wait(free_sem.at[x * 2 + 1 - core], 1)
            column_copy(0, 1 - core).start()

        @pl.when(part > 0)
        def _():
            for to_core in range(2):
                pl.semaphore_wait(free_sem.at[((x + chip_offset(part)) % 4) * 2 + to_core], 1)
                column_copy(part, to_core).start()

    def collect():
        column_home().wait()
        for step in range(1, 8):
            source = (att + step) % 8
            pltpu.make_async_copy(slots.at[0], slots.at[source], column_recv.at[source]).wait()
        gather_sent(RAW)
        lane = lax.broadcasted_iota(jnp.int32, (32, 128), 1)

        @pl.loop(0, 16)
        def _(i):
            of_y, of_z = i // 4, i % 4
            table = slot_table(of_y, of_z, lane)
            lines = slots[:, of_y, of_z].reshape(128, x_half)
            sums_of = jnp.dot(table, lines, preferred_element_type=F32).astype(BF16)
            for j in range(2):
                for k in range(2):
                    start = 32 * k + 16 * j
                    raw[of_y, of_z, :, pl.ds(extra * j + x_half * k, x_half)] = sums_of[start : start + 16]

    send_own(RAW)
    in_copy(0, 1 - core).start()
    for part in range(1, 4):
        for to_core in range(2):
            in_copy(part, to_core).start()
    rows[0, y, z, :, pl.ds(pl.multiple_of(core * g_half, 128), g_half)] = blocks_out[att]
    gather_own(0)
    gather_a(RAW)
    gather_b(RAW)
    gather_c(RAW)
    gather_d(RAW)

    def products(part, second):
        @pl.when(jnp.logical_not(second))
        def _():
            complete(part)
            free_slots(part)

        project(part, jnp.where(second, 2, 0))

    def lowering(part, second):
        @pl.when(jnp.logical_not(second))
        def _():
            activate()
            gather_sent(part)

        lower_rows(part, jnp.where(second, 2, 0))

        @pl.when(jnp.logical_not(second))
        def _():
            return_columns(part)

    def spread(part):
        for load in loads:
            load.wait()
        fill_slots()
        for part in range(3):
            shift(part)

    steps = [
        gather_own, gather_a, gather_b, gather_c, gather_d, gather_f, gather_e,
        products, products, lowering, lowering, reduce_1a, reduce_1b,
        *[functools.partial(reduce_2, pieces=(i,)) for i in range(4)],
        *[functools.partial(reduce_3, pieces=(i,)) for i in range(4)],
        reduce_5,
        lambda part: gather_f(RAW), lambda part: gather_e(RAW), spread, lambda part: shift(3),
        lambda part: collect(), lambda part: reduce_1a(RAW), lambda part: reduce_1b(RAW),
        *[lambda part, i=i: reduce_2(RAW, (i,)) for i in range(4)],
        *[lambda part, i=i: reduce_3(RAW, (i,)) for i in range(4)],
    ]

    def take(kind, part, low, high):
        if high - low == 1:
            steps[low](part)
        elif steps[low] is steps[high - 1]:
            steps[low](part, kind > low)
        else:
            middle = (low + high) // 2
            if steps[middle] is steps[middle - 1]:
                middle += 1
            lax.cond(
                kind < middle, lambda: take(kind, part, low, middle), lambda: take(kind, part, middle, high)
            )

    per_word = 3
    words = [sum(code << (8 * k) for k, code in enumerate(ORDER[i : i + per_word])) for i in range(0, len(ORDER), per_word)]

    @pl.loop(0, len(ORDER))
    def _(step):
        at = step // per_word
        word = jnp.int32(words[0])
        for i in range(1, len(words)):
            word = jnp.where(at == i, jnp.int32(words[i]), word)
        code = lax.shift_right_logical(word, 8 * (step % per_word)) % 256
        take(code // 4, code % 4, 0, len(steps))

    column_copy(0, 1 - core).wait_send()
    in_copy(0, 1 - core).wait_send()
    back_copy(0, 1 - core).wait_send()
    for part in range(1, 4):
        for to_core in range(2):
            column_copy(part, to_core).wait_send()
            in_copy(part, to_core).wait_send()
            back_copy(part, to_core).wait_send()
    for step in range(1, 8):
        source = (att + step) % 8
        pltpu.make_async_copy(blocks_back.at[0, 0], returned.at[source], back_recv.at[source]).wait()
    lines = returned[...].reshape(128, g_half)
    for table, cols in ((table_a, slice(0, g_half)), (table_b, slice(g_half, split))):
        found = lax.dot_general(table, lines, FIRST, preferred_element_type=F32)
        out[:, cols] = (hidden[:, cols].astype(F32) + found).astype(BF16)
    reduce_5(RAW)


def per_device(hidden, route, norm_gain, gate_weight, up_weight, down_weight):
    row_count, width = hidden.shape
    units = gate_weight.shape[2]
    extra = raw_columns(width)
    split = width - extra
    more = halves(split)[3][0].size
    vmem, dma = pltpu.VMEM, pltpu.SemaphoreType.DMA
    return pl.pallas_call(
        ffn_kernel,
        out_shape=jax.ShapeDtypeStruct((row_count, width), BF16),
        in_specs=[pl.BlockSpec(memory_space=pl.ANY)] + [pl.BlockSpec(memory_space=vmem)] * 2 + [pl.BlockSpec(memory_space=pl.ANY)] * 3,
        out_specs=pl.BlockSpec(memory_space=vmem),
        scratch_shapes=[
            vmem((units, width), BF16),
            vmem((units, width), BF16),
            vmem((units, width), BF16),
            vmem((8, 16, split // 2), BF16),
            vmem((4, 2, 16, split // 2), BF16),
            vmem((8, 16, split // 2), BF16),
            vmem((4, 4, 4, 16, width), BF16),
            vmem((4, 4, 16, 2 * extra + 256), BF16),
            vmem((8, 4, 4, 16, extra // 2), BF16),
            vmem((row_count, width), BF16),
            vmem((units, 256), F32),
            vmem((units, 256), F32),
            vmem((256, units), BF16),
            vmem((3, 2, 4, 16, more), BF16),
            vmem((3, 2, 4, 16, more), BF16),
            vmem((3, 2, 4, 16, split // 2), BF16),
            vmem((3, 2, 4, 16, split // 2), BF16),
            vmem((3, 2, 16, more), BF16),
            vmem((3, 2, 16, more), BF16),
            vmem((3, 2, 16, split // 2), BF16),
            vmem((3, 2, 16, split // 2), BF16),
            dma((3,)),
            dma((4, 2)),
            dma((4, 2)),
            dma((4, 2)),
            dma((4, 2)),
            dma,
            dma((4, 2)),
            dma((8,)),
            pltpu.SemaphoreType.REGULAR((8,)),
            dma((4, 2)),
            dma((8,)),
            dma((5, 9)),
            dma((5, 4, 9)),
            dma((5, 4)),
            dma((5, 4, 10)),
        ],
        compiler_params=pltpu.CompilerParams(
            collective_id=0, has_side_effects=True, vmem_limit_bytes=63 * 1024 * 1024
        ),
    )(
        hidden, route.reshape(1, row_count), norm_gain.reshape(1, width),
        jnp.swapaxes(gate_weight, 1, 2), jnp.swapaxes(up_weight, 1, 2), down_weight,
    )


def solution(mesh):
    placed = (
        P(("att", "ffn"), None),
        P(("att", "ffn"), None),
        P(),
        P("att", None, "ffn"),
        P("att", None, "ffn"),
        P("att", "ffn", None),
    )
    return jax.shard_map(
        per_device, mesh=mesh, in_specs=placed, out_specs=P(("att", "ffn"), None), check_vma=False
    )
```

```python
import functools

import jax
import jax.numpy as jnp
from jax import lax
from jax.experimental import pallas as pl
from jax.experimental.pallas import tpu as pltpu
from jax.sharding import PartitionSpec as P

MESH = pl.DeviceIdType.MESH
F32 = jnp.float32
BF16 = jnp.bfloat16
FIRST = (((0,), (0,)), ((), ()))
LAST = (((1,), (1,)), ((), ()))


RAW = 4

ORDER = (
    4, 88, 8, 1, 92, 12, 16, 96, 20, 5, 9, 2, 24, 28, 13, 17, 32, 21, 6, 36,
    10, 25, 100, 3, 40, 14, 29, 18, 33, 22, 7, 37, 41, 45, 49, 11, 26, 30, 53, 57,
    34, 15, 38, 19, 61, 23, 65, 42, 46, 50, 69, 27, 31, 54, 58, 62, 66, 44, 35, 48,
    39, 43, 70, 73, 77, 47, 51, 74, 78, 81, 85, 55, 59, 63, 67, 82, 71, 86, 52, 56,
    75, 79, 60, 64, 83, 104, 108, 112, 68, 116, 120, 124, 128, 87, 132, 72, 76, 80, 136, 140,
    144, 84,
)


def chip_offset(part):
    return part + part // 2 - 2 * (part // 3)


def raw_columns(width):
    return width // 4


def halves(width):
    half = width // 2
    more = (half // 128 + 1) // 2 * 128
    less = half - more
    quarters = [pl.ds(0, more), pl.ds(more, less), pl.ds(half, less), pl.ds(half + less, more)]
    return pl.ds(0, width), pl.ds(0, half), pl.ds(half, half), quarters


def ffn_kernel(
    hidden_hbm, route, gain, gate_hbm, up_hbm, down_hbm, out,
    w_gate, w_up, w_down, blocks_out, blocks_back, returned, rows, raw, slots, hidden,
    gate_sum, up_sum, mid,
    near_y1, near_z1, near_y2, near_z2, far_z1, far_y1, far_z2, far_y2,
    w_sem, in_send, in_recv, shift_send, shift_recv, home_sem, column_send, column_recv, free_sem, back_send, back_recv, gather_send, gather_recv, reduce_send, reduce_recv,
):
    att, ffn = lax.axis_index("att"), lax.axis_index("ffn")
    x, core = att // 2, att % 2
    y, z = ffn // 4, ffn % 4
    yp, y2, ym = (y + 1) % 4, (y + 2) % 4, (y + 3) % 4
    zp, z2, zm = (z + 1) % 4, (z + 2) % 4, (z + 3) % 4
    width = hidden_hbm.shape[1]
    quarter = width // 4
    extra = raw_columns(width)
    split = width - extra
    g_half, x_half = split // 2, extra // 2
    slot_geometry, raw_geometry, sum_geometry = halves(split), halves(2 * extra + 256), halves(2 * extra)
    z_plus, z_minus, y_plus, y_minus = (att, y * 4 + zp), (att, y * 4 + zm), (att, yp * 4 + z), (att, ym * 4 + z)
    ALL = pl.ds(0, 4)

    fetch = pltpu.make_async_copy(hidden_hbm, hidden, home_sem)
    fetch.start()
    barrier = pltpu.get_barrier_semaphore()
    for other in (z_plus, z_minus, y_plus, y_minus):
        pl.semaphore_signal(barrier, inc=1, device_id=other, device_id_type=MESH)
    for step in range(1, 8):
        pl.semaphore_signal(barrier, inc=1, device_id=((att + step) % 8, ffn), device_id_type=MESH)
    loads = [
        pltpu.make_async_copy(src.at[0], dst, w_sem.at[i])
        for i, (src, dst) in enumerate(((gate_hbm, w_gate), (up_hbm, w_up), (down_hbm, w_down)))
    ]
    for load in loads:
        load.start()

    fetch.wait()
    widened = hidden[...].astype(F32)
    scale = lax.rsqrt(jnp.mean(widened * widened, axis=-1, keepdims=True) + 1e-06)
    normed = (widened * scale * gain[...]).astype(BF16)
    member = (lax.broadcasted_iota(jnp.int32, (8, 32), 0) == route[...]).astype(F32)
    earlier = (
        lax.broadcasted_iota(jnp.int32, (32, 32), 0) < lax.broadcasted_iota(jnp.int32, (32, 32), 1)
    ).astype(F32)
    before = jnp.dot(member, earlier, preferred_element_type=F32)
    rank = jnp.sum(before * member, axis=0, keepdims=True).astype(jnp.int32)
    place = route[...] * 16 + rank
    line = lax.broadcasted_iota(jnp.int32, (128, 32), 0)
    table_a = (line == place).astype(F32).astype(BF16)
    table_b = (line == place + 8).astype(F32).astype(BF16)
    placed = jnp.dot(table_a, normed[:, :g_half], preferred_element_type=F32)
    placed = placed + jnp.dot(table_b, normed[:, g_half:split], preferred_element_type=F32)
    blocks_out[...] = placed.astype(BF16).reshape(8, 16, g_half)
    number = jnp.broadcast_to(place.astype(F32), (128, 32)).T.astype(BF16)
    for i in range(2):
        lines = slice(16 * i, 16 * i + 16)
        raw[y, z, :, extra * i : extra * (i + 1)] = normed[lines, split:]
        raw[y, z, :, 2 * extra + 128 * i : 2 * extra + 128 * (i + 1)] = number[lines]

    pl.semaphore_wait(barrier, 11)

    def arrival(part, from_core):
        return rows.at[part, y, z, :, pl.ds(pl.multiple_of(from_core * g_half, 128), g_half)]

    def in_copy(part, to_core):
        dest = ((x + 4 - chip_offset(part)) % 4) * 2 + to_core
        return pltpu.make_async_remote_copy(
            src_ref=blocks_out.at[dest], dst_ref=arrival(part, core),
            send_sem=in_send.at[part, to_core], recv_sem=in_recv.at[part, core],
            device_id=(dest, ffn), device_id_type=MESH,
        )

    def wait_in(part, from_core):
        pltpu.make_async_copy(blocks_out.at[0], arrival(part, from_core), in_recv.at[part, from_core]).wait()

    LINK = {0: z_plus, 1: z_minus, 2: y_plus, 3: y_minus}

    def geometry(part):
        return raw_geometry if part is RAW else slot_geometry

    def unit(part, at_y, at_z, cols):
        return raw.at[at_y, at_z, :, cols] if part is RAW else rows.at[part, at_y, at_z, :, cols]

    def g_send(part, link, event, at_y, at_z, cols):
        piece = unit(part, at_y, at_z, cols)
        pltpu.make_async_remote_copy(
            src_ref=piece, dst_ref=piece,
            send_sem=gather_send.at[part, event], recv_sem=gather_recv.at[part, link, event],
            device_id=LINK[link], device_id_type=MESH,
        ).start()

    def g_wait(part, link, event, cols):
        piece = unit(part, 0, 0, cols)
        pltpu.make_async_copy(piece, piece, gather_recv.at[part, link, event]).wait()

    def gather_own(part):
        @pl.when(part == 0)
        def _():
            wait_in(0, 1 - core)

        @pl.when(part > 0)
        def _():
            wait_in(part, 0)
            wait_in(part, 1)

        _, ga_cols, gb_cols, _ = slot_geometry
        first, second = rows[part, y, z, :, ga_cols].astype(F32), rows[part, y, z, :, gb_cols].astype(F32)
        rows[part, y, z, :, ga_cols] = jnp.concatenate([first[:8], second[:8]], axis=0).astype(BF16)
        rows[part, y, z, :, gb_cols] = jnp.concatenate([first[8:], second[8:]], axis=0).astype(BF16)
        send_own(part)

    def send_own(part):
        for link in range(4):
            g_send(part, link, 0, y, z, geometry(part)[0])

    def gather_a(part):
        whole, ga_cols, gb_cols, g = geometry(part)
        for link in range(4):
            g_wait(part, link, 0, whole)
        g_send(part, 0, 1, y, zm, g[0])
        g_send(part, 1, 1, y, zp, g[1])
        g_send(part, 2, 1, ym, z, g[2])
        g_send(part, 3, 1, yp, z, g[3])
        for link in (2, 3):
            g_send(part, link, 2, y, zm, ga_cols)
        for link in (0, 1):
            g_send(part, link, 2, ym, z, gb_cols)
        for link in (2, 3):
            g_send(part, link, 3, y, zp, ga_cols)
        for link in (0, 1):
            g_send(part, link, 3, yp, z, gb_cols)
        g_send(part, 0, 5, y, zm, g[2])
        g_send(part, 1, 5, y, zp, g[3])
        g_send(part, 2, 5, ym, z, g[0])
        g_send(part, 3, 5, yp, z, g[1])

    def gather_b(part):
        _, ga_cols, gb_cols, g = geometry(part)
        for link in range(4):
            g_wait(part, link, 1, g[link])
        for link in (2, 3):
            g_send(part, link, 4, y, z2, ga_cols)
        for link in (0, 1):
            g_send(part, link, 4, y2, z, gb_cols)

    def gather_on(part, event, of_y, of_z):
        _, ga_cols, _, g = geometry(part)
        for link in range(4):
            g_wait(part, link, event, ga_cols)
        g_send(part, 0, event + 4, of_y, zm, g[2])
        g_send(part, 1, event + 4, of_y, zp, g[3])
        g_send(part, 2, event + 4, ym, of_z, g[0])
        g_send(part, 3, event + 4, yp, of_z, g[1])

    def gather_c(part):
        gather_on(part, 2, ym, zm)

    def gather_d(part):
        gather_on(part, 3, yp, zp)

    def gather_f(part):
        gather_on(part, 4, y2, z2)

    def gather_e(part):
        g = geometry(part)[3]
        for event in range(5, 9):
            for link in range(4):
                g_wait(part, link, event, g[(link + 2) % 4])

    def gather_sent(part):
        for event, units in enumerate((4, 1, 2, 2, 2, 1, 1, 1, 1)):
            if part is RAW:
                piece = raw.at[0, pl.ds(0, units)]
            else:
                piece = rows.at[part, 0, pl.ds(0, units), :, slot_geometry[0]]
            pltpu.make_async_copy(piece, piece, gather_send.at[part, event]).wait()

    def slot_table(of_y, of_z, lane):
        where = jnp.concatenate([raw[of_y, of_z, :, pl.ds(2 * extra + 128 * j, 128)] for j in (0, 1)], axis=0)
        where = where.astype(F32).astype(jnp.int32)
        return jnp.concatenate([(lane == where).astype(F32), (lane == where + 8).astype(F32)], axis=0).astype(BF16)

    def fill_slots():
        lane = lax.broadcasted_iota(jnp.int32, (32, 128), 1)

        @pl.loop(0, 16)
        def _(i):
            of_y, of_z = i // 4, i % 4
            table = slot_table(of_y, of_z, lane)
            lines = [raw[of_y, of_z, :, pl.ds(extra * j + x_half * k, x_half)] for k in (0, 1) for j in (0, 1)]
            filled = lax.dot_general(table, jnp.concatenate(lines, axis=0), FIRST, preferred_element_type=F32)
            slots[:, of_y, of_z] = filled.astype(BF16).reshape(8, 16, x_half)

    def shifted(part, from_core):
        cols = pl.ds(pl.multiple_of(split + from_core * x_half, 128), x_half)
        return rows.at[part, :, :, :, cols]

    def shift_copy(part, to_core):
        dest = ((x + 4 - chip_offset(part)) % 4) * 2 + to_core
        return pltpu.make_async_remote_copy(
            src_ref=slots.at[dest], dst_ref=shifted(part, core),
            send_sem=shift_send.at[part, to_core], recv_sem=shift_recv.at[part, core],
            device_id=(dest, ffn), device_id_type=MESH,
        )

    def shift_home():
        return pltpu.make_async_copy(slots.at[att], shifted(0, core), home_sem)

    def shift(part):
        if part == 0:
            shift_home().start()
            shift_copy(0, 1 - core).start()
        else:
            shift_copy(part, 0).start()
            shift_copy(part, 1).start()

    def wait_shift(part, from_core):
        pltpu.make_async_copy(slots.at[0], shifted(part, from_core), shift_recv.at[part, from_core]).wait()

    def complete(part):
        @pl.when(part == 0)
        def _():
            shift_home().wait()
            wait_shift(0, 1 - core)

        @pl.when(part > 0)
        def _():
            wait_shift(part, 0)
            wait_shift(part, 1)

        complete_again(part)

    def complete_again(part):
        @pl.loop(0, 16)
        def _(i):
            of_y, of_z = i // 4, i % 4
            first = rows[part, of_y, of_z, :, split : split + x_half].astype(F32)
            second = rows[part, of_y, of_z, :, split + x_half :].astype(F32)
            rows[part, of_y, of_z, :, split : split + x_half] = (
                jnp.concatenate([first[:8], second[:8]], axis=0).astype(BF16)
            )
            rows[part, of_y, of_z, :, split + x_half :] = (
                jnp.concatenate([first[8:], second[8:]], axis=0).astype(BF16)
            )

    def project(part, lower):
        @pl.loop(lower, lower + 2)
        def _(i):
            cols = pl.ds(pl.multiple_of(i * quarter, quarter), quarter)
            block = rows[part, :, :, :, cols].reshape(256, quarter)
            gate = lax.dot_general(w_gate[:, cols], block, LAST, preferred_element_type=F32)
            up = lax.dot_general(w_up[:, cols], block, LAST, preferred_element_type=F32)

            @pl.when(i == 0)
            def _():
                gate_sum[...] = gate
                up_sum[...] = up

            @pl.when(i > 0)
            def _():
                gate_sum[...] += gate
                up_sum[...] += up

    def activate():
        gate = gate_sum[...]
        mid[...] = (gate / (1.0 + jnp.exp(-gate)) * up_sum[...]).T.astype(BF16)

    def lower_rows(part, lower):
        @pl.loop(lower, lower + 2)
        def _(step):
            cols = pl.ds(pl.multiple_of((3 - step) * quarter, quarter), quarter)
            partial = jnp.dot(mid[...], w_down[:, cols], preferred_element_type=F32)
            rows[part, :, :, :, cols] = partial.astype(BF16).reshape(4, 4, 16, quarter)

    def sums(part):
        return sum_geometry if part is RAW else slot_geometry

    def landing(part):
        return 1 if part is RAW else part * 2 // 3

    def place_at(buffer, part, cols, *index):
        return buffer.at[(landing(part), *index, slice(None), pl.ds(0, cols.size))]

    def r_send(part, link, event, src, dst):
        pltpu.make_async_remote_copy(
            src_ref=src, dst_ref=dst,
            send_sem=reduce_send.at[part, 3 if event == 9 else event // 4], recv_sem=reduce_recv.at[part, link, event],
            device_id=LINK[link], device_id_type=MESH,
        ).start()

    def r_wait(part, link, event, dst):
        pltpu.make_async_copy(dst, dst, reduce_recv.at[part, link, event]).wait()

    def add(piece, *terms):
        total = piece[...].astype(F32)
        for term in terms:
            total = total + term[...].astype(F32)
        piece[...] = total.astype(BF16)

    across_z, across_y = (z2, zp, zm, z), (y2, yp, ym, y)

    def reduce_1a(part):
        q = sums(part)[3]
        for i in range(4):
            for side in range(2):
                cols = q[side]
                r_send(part, 2 + side, i, unit(part, y2, across_z[i], cols), place_at(near_y1, part, cols, side, i))

    def reduce_1b(part):
        q = sums(part)[3]
        for i in range(4):
            for side in range(2):
                cols = q[2 + side]
                r_send(part, side, i, unit(part, across_y[i], z2, cols), place_at(near_z1, part, cols, side, i))

    def reduce_2(part, pieces):
        _, a_cols, b_cols, q = sums(part)
        for i in pieces:
            at_y, at_z = across_y[i], across_z[i]
            for side, goal in ((0, yp), (1, ym)):
                landed = place_at(near_y1, part, q[side], side, i)
                r_wait(part, 2 + side, i, landed)
                add(unit(part, goal, at_z, q[side]), landed)
                r_send(part, 2 + side, 4 + i, unit(part, goal, at_z, a_cols), place_at(near_y2, part, a_cols, side, i))
            for side, goal in ((0, zp), (1, zm)):
                landed = place_at(near_z1, part, q[2 + side], side, i)
                r_wait(part, side, i, landed)
                add(unit(part, at_y, goal, q[2 + side]), landed)
                r_send(part, side, 4 + i, unit(part, at_y, goal, b_cols), place_at(near_z2, part, b_cols, side, i))

    def reduce_3(part, pieces):
        _, a_cols, b_cols, q = sums(part)
        for i in pieces:
            at_y, at_z = across_y[i], across_z[i]
            landed = [place_at(near_y2, part, a_cols, side, i) for side in range(2)]
            r_wait(part, 2, 4 + i, landed[0])
            r_wait(part, 3, 4 + i, landed[1])
            add(unit(part, y, at_z, a_cols), *landed)
            landed = [place_at(near_z2, part, b_cols, side, i) for side in range(2)]
            r_wait(part, 0, 4 + i, landed[0])
            r_wait(part, 1, 4 + i, landed[1])
            add(unit(part, at_y, z, b_cols), *landed)
            if i == 0:
                for side in range(2):
                    r_send(part, side, 8, unit(part, y, z2, q[side]), place_at(far_z1, part, q[side], side))
                    cols = q[2 + side]
                    r_send(part, 2 + side, 8, unit(part, y2, z, cols), place_at(far_y1, part, cols, side))
            elif i < 3:
                side = i - 1
                landed = place_at(far_z1, part, q[side], side)
                r_wait(part, side, 8, landed)
                add(unit(part, y, at_z, q[side]), landed)
                r_send(part, side, 9, unit(part, y, at_z, a_cols), place_at(far_z2, part, a_cols, side))
                landed = place_at(far_y1, part, q[2 + side], side)
                r_wait(part, 2 + side, 8, landed)
                add(unit(part, at_y, z, q[2 + side]), landed)
                r_send(part, 2 + side, 9, unit(part, at_y, z, b_cols), place_at(far_y2, part, b_cols, side))

    def back_copy(part, to_core):
        dest = ((x + chip_offset(part)) % 4) * 2 + to_core
        return pltpu.make_async_remote_copy(
            src_ref=blocks_back.at[part, to_core], dst_ref=returned.at[att],
            send_sem=back_send.at[part, to_core], recv_sem=back_recv.at[att],
            device_id=(dest, ffn), device_id_type=MESH,
        )

    def reduce_5(part):
        whole, a_cols, b_cols, _ = sums(part)
        left, right = unit(part, y, z, a_cols)[...].astype(F32), unit(part, y, z, b_cols)[...].astype(F32)
        for side in range(2):
            landed = place_at(far_z2, part, a_cols, side)
            r_wait(part, side, 9, landed)
            left = left + landed[...].astype(F32)
            landed = place_at(far_y2, part, b_cols, side)
            r_wait(part, 2 + side, 9, landed)
            right = right + landed[...].astype(F32)
        if part is RAW:
            out[:16, split:] = (hidden[:16, split:].astype(F32) + left.astype(BF16).astype(F32)).astype(BF16)
            out[16:, split:] = (hidden[16:, split:].astype(F32) + right.astype(BF16).astype(F32)).astype(BF16)
        else:
            for to_core in range(2):
                lines = slice(8 * to_core, 8 * to_core + 8)
                blocks_back[part, to_core] = jnp.concatenate([left[lines], right[lines]], axis=0).astype(BF16)

            @pl.when(part == 0)
            def _():
                back_copy(part, 1 - core).start()
                returned[att] = blocks_back[part, core]

            @pl.when(part > 0)
            def _():
                back_copy(part, 0).start()
                back_copy(part, 1).start()

        for event, units in enumerate((4, 8, 1, 2)):
            many = (0, pl.ds(0, units)) if units <= 4 else (pl.ds(0, units // 4),)
            if part is RAW:
                piece = raw_units(many, whole)
            else:
                piece = part_units(part, many, whole)
            pltpu.make_async_copy(piece, piece, reduce_send.at[part, event]).wait()

    def raw_units(many, cols):
        return raw.at[many[0], many[1], :, cols] if len(many) == 2 else raw.at[many[0], :, :, cols]

    def part_units(part, many, cols):
        return rows.at[part, many[0], many[1], :, cols] if len(many) == 2 else rows.at[part, many[0], :, :, cols]

    def column_copy(part, to_core):
        dest = ((x + chip_offset(part)) % 4) * 2 + to_core
        return pltpu.make_async_remote_copy(
            src_ref=shifted(part, to_core), dst_ref=slots.at[att],
            send_sem=column_send.at[part, to_core], recv_sem=column_recv.at[att],
            device_id=(dest, ffn), device_id_type=MESH,
        )

    def column_home():
        return pltpu.make_async_copy(shifted(0, core), slots.at[att], home_sem)

    def free_slots(part):
        def free(to_core):
            dest = ((x + 4 - chip_offset(part)) % 4) * 2 + to_core
            shift_copy(part, to_core).wait_send()
            pl.semaphore_signal(free_sem.at[att], inc=1, device_id=(dest, ffn), device_id_type=MESH)

        @pl.when(part == 0)
        def _():
            free(1 - core)

        @pl.when(part > 0)
        def _():
            free(0)
            free(1)

    def return_columns(part):
        complete_again(part)

        @pl.when(part == 0)
        def _():
            column_home().start()
            pl.semaphore_wait(free_sem.at[x * 2 + 1 - core], 1)
            column_copy(0, 1 - core).start()

        @pl.when(part > 0)
        def _():
            for to_core in range(2):
                pl.semaphore_wait(free_sem.at[((x + chip_offset(part)) % 4) * 2 + to_core], 1)
                column_copy(part, to_core).start()

    def collect():
        column_home().wait()
        for step in range(1, 8):
            source = (att + step) % 8
            pltpu.make_async_copy(slots.at[0], slots.at[source], column_recv.at[source]).wait()
        gather_sent(RAW)
        lane = lax.broadcasted_iota(jnp.int32, (32, 128), 1)

        @pl.loop(0, 16)
        def _(i):
            of_y, of_z = i // 4, i % 4
            table = slot_table(of_y, of_z, lane)
            lines = slots[:, of_y, of_z].reshape(128, x_half)
            sums_of = jnp.dot(table, lines, preferred_element_type=F32).astype(BF16)
            for j in range(2):
                for k in range(2):
                    start = 32 * k + 16 * j
                    raw[of_y, of_z, :, pl.ds(extra * j + x_half * k, x_half)] = sums_of[start : start + 16]

    send_own(RAW)
    in_copy(0, 1 - core).start()
    for part in range(1, 4):
        for to_core in range(2):
            in_copy(part, to_core).start()
    rows[0, y, z, :, pl.ds(pl.multiple_of(core * g_half, 128), g_half)] = blocks_out[att]
    gather_own(0)
    gather_a(RAW)
    gather_b(RAW)
    gather_c(RAW)
    gather_d(RAW)

    def products(part, second):
        @pl.when(jnp.logical_not(second))
        def _():
            complete(part)
            free_slots(part)

        project(part, jnp.where(second, 2, 0))

    def lowering(part, second):
        @pl.when(jnp.logical_not(second))
        def _():
            activate()
            gather_sent(part)

        lower_rows(part, jnp.where(second, 2, 0))

        @pl.when(jnp.logical_not(second))
        def _():
            return_columns(part)

    def spread(part):
        for load in loads:
            load.wait()
        fill_slots()
        for part in range(3):
            shift(part)

    steps = [
        gather_own, gather_a, gather_b, gather_c, gather_d, gather_f, gather_e,
        products, products, lowering, lowering, reduce_1a, reduce_1b,
        *[functools.partial(reduce_2, pieces=(i,)) for i in range(4)],
        *[functools.partial(reduce_3, pieces=(i,)) for i in range(4)],
        reduce_5,
        lambda part: gather_f(RAW), lambda part: gather_e(RAW), spread, lambda part: shift(3),
        lambda part: collect(), lambda part: reduce_1a(RAW), lambda part: reduce_1b(RAW),
        *[lambda part, i=i: reduce_2(RAW, (i,)) for i in range(4)],
        *[lambda part, i=i: reduce_3(RAW, (i,)) for i in range(4)],
    ]

    def take(kind, part, low, high):
        if high - low == 1:
            steps[low](part)
        elif steps[low] is steps[high - 1]:
            steps[low](part, kind > low)
        else:
            middle = (low + high) // 2
            if steps[middle] is steps[middle - 1]:
                middle += 1
            lax.cond(
                kind < middle, lambda: take(kind, part, low, middle), lambda: take(kind, part, middle, high)
            )

    per_word = 4
    words = [sum(code << (8 * k) for k, code in enumerate(ORDER[i : i + per_word])) for i in range(0, len(ORDER), per_word)]
    words = [word - (1 << 32) if word >= 1 << 31 else word for word in words]

    @pl.loop(0, len(ORDER))
    def _(step):
        at = step // per_word
        left = [jnp.int32(word) for word in words]
        while len(left) > 1:
            odd = at % 2 == 1
            left = [jnp.where(odd, *left[i : i + 2][::-1]) if i + 1 < len(left) else left[i] for i in range(0, len(left), 2)]
            at = at // 2
        code = lax.shift_right_logical(left[0], 8 * (step % per_word)) % 256
        take(code // 4, code % 4, 0, len(steps))

    column_copy(0, 1 - core).wait_send()
    in_copy(0, 1 - core).wait_send()
    back_copy(0, 1 - core).wait_send()
    for part in range(1, 4):
        for to_core in range(2):
            column_copy(part, to_core).wait_send()
            in_copy(part, to_core).wait_send()
            back_copy(part, to_core).wait_send()
    for step in range(1, 8):
        source = (att + step) % 8
        pltpu.make_async_copy(blocks_back.at[0, 0], returned.at[source], back_recv.at[source]).wait()
    lines = returned[...].reshape(128, g_half)
    for table, cols in ((table_a, slice(0, g_half)), (table_b, slice(g_half, split))):
        found = lax.dot_general(table, lines, FIRST, preferred_element_type=F32)
        out[:, cols] = (hidden[:, cols].astype(F32) + found).astype(BF16)
    reduce_5(RAW)


def per_device(hidden, route, norm_gain, gate_weight, up_weight, down_weight):
    row_count, width = hidden.shape
    units = gate_weight.shape[2]
    extra = raw_columns(width)
    split = width - extra
    more = halves(split)[3][0].size
    vmem, dma = pltpu.VMEM, pltpu.SemaphoreType.DMA
    return pl.pallas_call(
        ffn_kernel,
        out_shape=jax.ShapeDtypeStruct((row_count, width), BF16),
        in_specs=[pl.BlockSpec(memory_space=pl.ANY)] + [pl.BlockSpec(memory_space=vmem)] * 2 + [pl.BlockSpec(memory_space=pl.ANY)] * 3,
        out_specs=pl.BlockSpec(memory_space=vmem),
        scratch_shapes=[
            vmem((units, width), BF16),
            vmem((units, width), BF16),
            vmem((units, width), BF16),
            vmem((8, 16, split // 2), BF16),
            vmem((4, 2, 16, split // 2), BF16),
            vmem((8, 16, split // 2), BF16),
            vmem((4, 4, 4, 16, width), BF16),
            vmem((4, 4, 16, 2 * extra + 256), BF16),
            vmem((8, 4, 4, 16, extra // 2), BF16),
            vmem((row_count, width), BF16),
            vmem((units, 256), F32),
            vmem((units, 256), F32),
            vmem((256, units), BF16),
            vmem((3, 2, 4, 16, more), BF16),
            vmem((3, 2, 4, 16, more), BF16),
            vmem((3, 2, 4, 16, split // 2), BF16),
            vmem((3, 2, 4, 16, split // 2), BF16),
            vmem((3, 2, 16, more), BF16),
            vmem((3, 2, 16, more), BF16),
            vmem((3, 2, 16, split // 2), BF16),
            vmem((3, 2, 16, split // 2), BF16),
            dma((3,)),
            dma((4, 2)),
            dma((4, 2)),
            dma((4, 2)),
            dma((4, 2)),
            dma,
            dma((4, 2)),
            dma((8,)),
            pltpu.SemaphoreType.REGULAR((8,)),
            dma((4, 2)),
            dma((8,)),
            dma((5, 9)),
            dma((5, 4, 9)),
            dma((5, 4)),
            dma((5, 4, 10)),
        ],
        compiler_params=pltpu.CompilerParams(
            collective_id=0, has_side_effects=True, vmem_limit_bytes=63 * 1024 * 1024
        ),
    )(
        hidden, route.reshape(1, row_count), norm_gain.reshape(1, width),
        jnp.swapaxes(gate_weight, 1, 2), jnp.swapaxes(up_weight, 1, 2), down_weight,
    )


def solution(mesh):
    placed = (
        P(("att", "ffn"), None),
        P(("att", "ffn"), None),
        P(),
        P("att", None, "ffn"),
        P("att", None, "ffn"),
        P("att", "ffn", None),
    )
    return jax.shard_map(
        per_device, mesh=mesh, in_specs=placed, out_specs=P(("att", "ffn"), None), check_vma=False
    )
```
